32 devices in a mesh: groups: 2 (over x), shard: 8 (over z, y), tensor: 2 (over core).
Axes of the slice: x: 2, y: 2, z: 4, core: 2. Of those that a mesh axis runs over, the one named last changes fastest.
Arguments:
- hidden: bfloat16 [2048, 16384], P(('groups', 'shard'), 'tensor'), parts along dimension 0, may hold values from -6 to 6
- codes: bfloat16 [16384, 1024], P('tensor', 'shard'), may hold values from -448 to 448
- scales: float32 [128, 8], P('tensor'), may hold values from 3.6621095e-05 to 0.00036621094
- queries: bfloat16 [2048, 8192], P(('groups', 'shard'), 'tensor'), parts along dimension 0, may hold values from -160 to 160
- segment_ids: int32 [2048], P(('groups', 'shard')), parts along dimension 0, may hold values from 0 to 2, never falling along the last dimension, each value on 1 to 640 neighbouring positions
Outputs:
- attended: bfloat16 [2048, 8192], P(('groups', 'shard'), 'tensor'), parts along dimension 0
The draws below stay inside these ranges and needn't reach their ends.
There are 2 independent parts, one for each index of `groups`. The reference program is written for one: setup_inputs(seed, part) draws one part's arguments, and reference() takes and returns one part's arrays. A program takes and returns all parts, laid end to end along the dimension named above; an argument that names none is the same for every part. Nothing has to cross between parts.
All inputs are finite; a program needn't handle non-finite values.
Results may differ from the reference program's by a relative error of at most 0.006.
The reference program's roundings to bfloat16 on the way (of `weight`, `keyval` and `weights`) count: a program that leaves them out, or rounds other values in their place, can miss the bound.
Values may be sent and summed in bfloat16 or wider, within the bound.
No kernel may reach another device: no remote copies, remote signals or barrier semaphores. Data moves between devices by JAX's collectives and lax.ppermute only.
A program may use at most 192 MiB of HBM per device.

```python
import math
import jax
import jax.numpy as jnp
import numpy as np
from jax import lax

D = 16384
KVH = 4
HD = 128
QPK = 16
BLK = 128
SEGMAX = 640
QH = 64
KVW = 1024
TOKENS = 1024
SEGS = 3


def draw_queries(key, part):
    key = jax.random.fold_in(key, 11)
    base = jax.random.normal(key, (TOKENS, QH * HD), jnp.float32)
    return jnp.clip(base, -6.0, 6.0).astype(jnp.bfloat16)


def steps_of(stream_key, extent, cuts, least, high):
    factor_of = 1.0
    for axis_at, parts in cuts:
        heights = jax.random.uniform(jax.random.fold_in(jax.random.fold_in(stream_key, 6), axis_at), (parts,), jnp.float32, least / len(cuts), high / len(cuts))
        factor_of = factor_of * jnp.repeat(jnp.exp(heights), extent[axis_at] // parts).reshape((-1,) + (1,) * (len(extent) - 1 - axis_at))
    return factor_of


def length_profile(count, total, limit, skew):
    loads = [(1 << 20) // math.isqrt(grade ** skew) + 1 for grade in range(2, count + 1)]
    spare, holding = total - limit - (count - 1), [1] * (count - 1)
    while spare > 0:
        movable = [i for i in range(count - 1) if holding[i] < limit]
        whole, left = sum([loads[i] for i in movable]), spare
        for i in movable:
            more = min(limit - holding[i], max(1, left * loads[i] // whole), spare)
            holding[i] = holding[i] + more
            spare = spare - more
    return np.array([limit] + holding)


def ragged(key, count, total, limit, lean):
    if count == 2:
        one = jax.random.randint(key, (), max(1, total - limit), min(limit, total - 1) + 1)
        return jnp.stack([one, total - one])
    sizes = jnp.asarray(length_profile(count, total, limit, lean), jnp.int32)
    twos = (count - 1) // 2
    source_of, taker = sizes[1:1 + 2 * twos:2], sizes[2:2 + 2 * twos:2]
    slack = jnp.minimum(source_of - 1, limit - taker)
    moved = jax.random.randint(jax.random.fold_in(key, 1), (twos,), 0, 1 << 20) % (slack + 1)
    sizes = sizes.at[1:1 + 2 * twos:2].set(source_of - moved).at[2:2 + 2 * twos:2].set(taker + moved)
    return sizes[jax.random.permutation(jax.random.fold_in(key, 2), count)]


def scatter_about(rng, shape, scale, reach, split=(), kind=jnp.bfloat16):
    factor_of = steps_of(rng, shape, split, -0.22, 0.18) if split else 1.0
    values = jax.random.normal(rng, shape, jnp.float32) * scale * factor_of
    return jnp.minimum(jnp.maximum(values, -reach), reach).astype(kind)


def setup_inputs(seed: int = 0, part: int = 0) -> dict:
    keys = jax.random.split(jax.random.key(seed), 6)
    part_keys = jax.random.split(jax.random.fold_in(keys[5], part), 6)
    hidden = scatter_about(part_keys[0], (TOKENS, D), 1.0, 6.0, ((0, 8), (1, 2)))
    codes = scatter_about(keys[1], (D, KVW), 64.0, 448.0, ((0, 2), (1, 8)))
    scales = jnp.clip(jnp.exp(math.log(0.00036621094) - 2.3025851 * jax.random.uniform(keys[2], (D // BLK, KVW // BLK), jnp.float32) ** steps_of(keys[2], (D // BLK, KVW // BLK), ((0, 2),), -0.2, 0.2)), 3.662109520519152e-05, 0.00036621094)
    queries = draw_queries(jax.random.fold_in(jax.random.fold_in(keys[5], part), 71), part)
    segment_ids = jnp.searchsorted(jnp.cumsum(ragged(part_keys[4], SEGS, TOKENS, SEGMAX, 2)), jnp.arange(TOKENS), side="right").astype(jnp.int32)
    return dict(hidden=hidden, codes=codes, scales=scales, queries=queries, segment_ids=segment_ids)


def reference(hidden, codes, scales, queries, segment_ids):
    expand = jnp.repeat(jnp.repeat(scales, BLK, axis=0), BLK, axis=1)
    weight = (codes.astype(jnp.float32) * expand).astype(jnp.bfloat16)
    keyval = jnp.dot(hidden, weight, preferred_element_type=jnp.float32).astype(jnp.bfloat16)
    keyval = lax.optimization_barrier(keyval)
    packed = keyval.reshape(TOKENS, KVH, 2, HD)
    key_pad = jnp.concatenate([jnp.zeros((SEGMAX, KVH, HD), jnp.bfloat16), packed[:, :, 0, :]], axis=0)
    val_pad = jnp.concatenate([jnp.zeros((SEGMAX, KVH, HD), jnp.bfloat16), packed[:, :, 1, :]], axis=0)
    seg_pad = jnp.concatenate([jnp.full((SEGMAX,), -1, jnp.int32), segment_ids.astype(jnp.int32)], axis=0)
    query_all = queries.reshape(TOKENS, KVH, QPK, HD)
    qblock = math.gcd(TOKENS, 512)
    window = qblock + SEGMAX
    scaling = 1.0 / math.sqrt(HD)

    def block(index):
        start = (index * qblock).astype(jnp.int32)
        qpart = lax.dynamic_slice_in_dim(query_all, start, qblock, 0).astype(jnp.float32)
        kpart = lax.dynamic_slice_in_dim(key_pad, start, window, 0).astype(jnp.float32)
        vpart = lax.dynamic_slice_in_dim(val_pad, start, window, 0).astype(jnp.float32)
        spart = lax.dynamic_slice_in_dim(seg_pad, start, window, 0)
        sq = lax.dynamic_slice_in_dim(segment_ids.astype(jnp.int32), start, qblock, 0)
        scores = jnp.einsum('qgph,kgh->gpqk', qpart, kpart) * scaling
        rowpos = start + jnp.arange(qblock, dtype=jnp.int32)
        colpos = start - SEGMAX + jnp.arange(window, dtype=jnp.int32)
        allowed = (sq[:, None] == spart[None, :]) & (colpos[None, :] <= rowpos[:, None])
        scores = jnp.where(allowed[None, None], scores, -jnp.inf)
        top = lax.optimization_barrier(jnp.max(scores, axis=-1))
        weights = jnp.exp(scores - top[..., None])
        totals = lax.optimization_barrier(jnp.sum(weights, axis=-1))
        rounded = lax.optimization_barrier(weights.astype(jnp.bfloat16))
        summed = jnp.einsum('gpqk,kgh->qgph', rounded.astype(jnp.float32), vpart)
        result = summed / jnp.transpose(totals, (2, 0, 1))[..., None]
        return result.astype(jnp.bfloat16).reshape(qblock, QH * HD)
    blocks = lax.map(block, jnp.arange(TOKENS // qblock, dtype=jnp.int32))
    return blocks.reshape(TOKENS, QH * HD)
```

```python
import functools
import math

import jax
import jax.numpy as jnp
from jax import lax
from jax.experimental import pallas as pl
from jax.experimental.pallas import tpu as pltpu
from jax.sharding import Mesh
from jax.sharding import PartitionSpec as P

KVH = 4
HD = 128
QPK = 16
BLK = 128
KVW = 1024
PAD = 16
ALL = ("groups", "hi", "lo", "tensor")
BLOCK = ("groups", "lo")
SHARD = ("hi", "lo")
VMEM_LIMIT = 56 * 2**20


def flat_pairs(sizes, move):
    groups, shards, cores = sizes
    pairs = []
    for g in range(groups):
        for s in range(shards):
            for c in range(cores):
                to = move(g, s, c)
                if to is not None:
                    pairs.append(((g * shards + s) * cores + c, (to[0] * shards + to[1]) * cores + to[2]))
    return pairs


def turns_of(sizes, low, depth):
    if (sizes[0], low) != (2, 4) or depth % 128 or depth < 384:
        return None
    first = 128 * ((depth // 128 + 2) // 3)
    turns, start = [], 0
    for turn, width in enumerate((first, first, depth - 2 * first)):
        turns.append((start, width, tuple((turn + step) % 3 for step in range(3))))
        start += 8 * width
    return turns


def slice_index(place, axes):
    return place[axes[0]] * 4 + place[axes[1]] * 2 + place[axes[2]]


def scale_kernel(turns, place_ref, codes_ref, scales_ref, ids_ref, out_ref):
    lows = 4
    for lo in range(lows):
        place, at = (place_ref[0], lo // 2, lo % 2), 0
        for start, width, axes in turns:
            first = start + slice_index(place, axes) * width
            for k in range(width // BLK):
                row = pl.multiple_of(first + k * BLK, BLK)
                scale = scales_ref[row // BLK, place_ref[4]]
                block = codes_ref[pl.ds(row, BLK), :].astype(jnp.float32) * scale
                block = block.astype(jnp.bfloat16)
                for copy in range(lo, out_ref.shape[0], lows):
                    out_ref[copy, at : at + BLK, :] = block
                at += BLK
        for copy in range(lo, out_ref.shape[0], lows):
            out_ref[copy, at:, :] = ids_ref[...]


def scaled_weight(turns, place, low, shards, codes, scales, ids):
    group, column = place[0], place[4]
    width = codes.shape[1]
    if turns is not None and width == BLK:
        depth = sum(turn[1] for turn in turns)
        return pl.pallas_call(
            functools.partial(scale_kernel, turns),
            in_specs=[
                pl.BlockSpec(memory_space=pltpu.SMEM),
                pl.BlockSpec(memory_space=pltpu.VMEM),
                pl.BlockSpec(memory_space=pltpu.SMEM),
                pl.BlockSpec(memory_space=pltpu.VMEM),
            ],
            out_specs=pl.BlockSpec(memory_space=pltpu.VMEM),
            out_shape=jax.ShapeDtypeStruct((shards, depth + PAD, width), jnp.bfloat16),
            compiler_params=pltpu.CompilerParams(vmem_limit_bytes=VMEM_LIMIT),
            name="scale",
        )(place, codes, scales, ids)
    features = codes.shape[0]
    groups = lax.axis_size("groups")
    depth = features // (groups * low)
    if turns is not None:
        rows = []
        for lo in range(low):
            for start, size, axes in turns:
                first = start + slice_index((group, lo // 2, lo % 2), axes) * size
                rows.append(first + jnp.arange(size, dtype=jnp.int32))
        rows = jnp.concatenate(rows)
    else:
        rows = group * low * depth + jnp.arange(low * depth, dtype=jnp.int32)
    scale = lax.dynamic_slice_in_dim(scales, column, 1, 1)[rows // BLK]
    weight = (codes[rows].astype(jnp.float32) * scale).astype(jnp.bfloat16)
    weight = weight.reshape(low, depth, width)
    weight = jnp.concatenate([weight, jnp.broadcast_to(ids, (low, PAD, width))], axis=1)
    weight = jnp.broadcast_to(weight[None], (shards // low, low, depth + PAD, width))
    return weight.reshape(shards, depth + PAD, width)


def spread_hidden(turns, place, sizes, low, hidden):
    members = sizes[0] * low
    rows, features = hidden.shape
    depth = features // members
    if turns is None:
        sliced = jnp.moveaxis(hidden.reshape(rows, members, depth), 1, 0)
        got = lax.all_to_all(sliced, BLOCK, 0, 0, tiled=True).reshape(members * rows, depth)
        return [got], [(0, m * rows, None, depth, m, 0) for m in range(members)]
    moves = (
        lambda g, s, c: (1 - g, s, c),
        lambda g, s, c: (g, s ^ 2, c),
        lambda g, s, c: (g, s ^ 1, c),
    )
    bits = (4, 2, 1)
    states = []
    for start, width, axes in turns:
        states.append([(hidden, start, [0])])
    for step in range(3):
        for (start, width, axes), state in zip(turns, states):
            axis = axes[step]
            size = width * (4 >> step)
            here = place[axis]
            sends = [
                lax.dynamic_slice_in_dim(array, first + (1 - here) * size, size, 1)
                for array, first, _ in state
            ]
            got = lax.ppermute(
                jnp.concatenate(sends, axis=0) if len(sends) > 1 else sends[0],
                ALL,
                flat_pairs(sizes, moves[axis]),
            )
            distances = [b | bits[axis] for _, _, held in state for b in held]
            state[:] = [(array, first + here * size, held) for array, first, held in state]
            state.append((got, 0, distances))
    arrays, copies, column = [hidden], [], 0
    for (start, width, axes), state in zip(turns, states):
        for array, first, held in state:
            if array is not hidden:
                arrays.append(array)
            at = 0 if array is hidden else len(arrays) - 1
            for k, distance in enumerate(held):
                copies.append((at, k * rows, first, width, distance, column))
        column += width
    return arrays, copies


def project_kernel(copies, sources, wide, firsts_ref, place_ref, *refs):
    hidden_refs, (weight_ref, other_ref, mine_ref, left, halves, sems) = refs[:sources], refs[sources:]
    step = pl.program_id(0)
    rows = mine_ref.shape[1]
    depth, columns = halves.shape[1:]
    core, member = place_ref[3], place_ref[5]

    @pl.when(step == 0)
    def _():
        started = []
        for k, (at, row, _, width, distance, column) in enumerate(copies):
            first = pl.multiple_of(firsts_ref[k], 128)
            block = distance if wide else jnp.bitwise_xor(member, distance)
            to = pl.multiple_of(block * rows, rows)
            started.append(
                pltpu.make_async_copy(
                    hidden_refs[at].at[pl.ds(row, rows), pl.ds(first, width)],
                    left.at[pl.ds(to, rows), pl.ds(column, width)],
                    sems.at[k],
                )
            )
        shards = weight_ref.shape[0]
        width = weight_ref.shape[2]
        for s in range(shards):
            half = jnp.bitwise_xor(core, s * width // columns)
            started.append(
                pltpu.make_async_copy(
                    weight_ref.at[s, pl.ds(0, depth), :],
                    halves.at[half, :, pl.ds(s * width % columns, width)],
                    sems.at[len(copies) + s],
                )
            )
        for copy in started:
            copy.start()
        for copy in started:
            copy.wait()

    size = mine_ref.shape[2]
    per_half = columns // size
    for half, out_ref in ((1, other_ref), (0, mine_ref)):
        for k in range(per_half):

            @pl.when(step == (1 - half) * per_half + k)
            def _():
                total = jnp.dot(
                    left[...],
                    halves[half, :, k * size : (k + 1) * size],
                    preferred_element_type=jnp.float32,
                )
                out_ref[...] = total.reshape(out_ref.shape)


def project(turns, arrays, copies, weight, place):
    members = max(copy[4] for copy in copies) + 1
    rows = arrays[0].shape[0] if turns is not None else arrays[0].shape[0] // members
    shards, deep, width = weight.shape
    depth = deep - PAD
    columns = shards * width // 2
    if width % 128:
        weight = jnp.moveaxis(weight[:, :depth].reshape(2, shards // 2, depth, width), 1, 2)
        weight = weight.reshape(2, depth, columns)
    firsts = jnp.stack([jnp.asarray(0 if c[2] is None else c[2], jnp.int32) for c in copies])
    size = 256
    per_half = columns // size
    out = jax.ShapeDtypeStruct((members, rows, columns), jnp.float32)
    return pl.pallas_call(
        functools.partial(project_kernel, copies, len(arrays), turns is None),
        grid_spec=pltpu.PrefetchScalarGridSpec(
            num_scalar_prefetch=2,
            grid=(2 * per_half,),
            in_specs=[pl.BlockSpec(memory_space=pl.ANY)] * (len(arrays) + 1),
            out_specs=[
                pl.BlockSpec((members, rows, size), lambda i, f, p: (0, 0, jnp.minimum(i, per_half - 1))),
                pl.BlockSpec((members, rows, size), lambda i, f, p: (0, 0, jnp.maximum(i - per_half, 0))),
            ],
            scratch_shapes=[
                pltpu.VMEM((members * rows, depth), jnp.bfloat16),
                pltpu.VMEM((2, depth, columns), jnp.bfloat16),
                pltpu.SemaphoreType.DMA((len(copies) + weight.shape[0],)),
            ],
        ),
        out_shape=[out, out],
        compiler_params=pltpu.CompilerParams(vmem_limit_bytes=VMEM_LIMIT),
        name="project",
    )(firsts, place, *arrays, weight)


def split_kernel(mine_ref, got_ref, out_ref):
    total = mine_ref[...] + got_ref[...]
    columns = total.shape[2]
    out_ref[:, :, :columns] = total.astype(jnp.bfloat16)
    for head in range(columns // (2 * HD)):
        keys = total[:, :, 2 * head * HD : (2 * head + 1) * HD]
        rest = keys - keys.astype(jnp.bfloat16).astype(jnp.float32)
        at = columns + head * HD
        out_ref[:, :, at : at + HD] = rest.astype(jnp.bfloat16)


def split(mine, got):
    members, rows, columns = mine.shape
    spec = pl.BlockSpec((2, rows, columns), lambda i: (i, 0, 0))
    wide = columns + columns // 2
    return pl.pallas_call(
        split_kernel,
        grid=(members // 2,),
        in_specs=[spec, spec],
        out_specs=pl.BlockSpec((2, rows, wide), lambda i: (i, 0, 0)),
        out_shape=jax.ShapeDtypeStruct((members, rows, wide), jnp.bfloat16),
        compiler_params=pltpu.CompilerParams(vmem_limit_bytes=VMEM_LIMIT),
        name="split",
    )(mine, got)


def attend_kernel(pieces, heads, stack, query_ref, allowed_ref, *refs):
    kv_refs, (out_ref, keys, values) = refs[:pieces], refs[pieces:]
    rows = query_ref.shape[0]
    scaling = 1.0 / math.sqrt(HD)
    for d, ref in enumerate(kv_refs):
        keys[d * rows : (d + 1) * rows, :] = ref[:, :HD]
        values[d * rows : (d + 1) * rows, :] = ref[:, HD:]
    allowed = allowed_ref[...]
    allowed = jnp.concatenate([allowed] * stack, axis=0) > 0.0
    for part in range(heads // stack):
        columns = [slice((part * stack + h) * HD, (part * stack + h + 1) * HD) for h in range(stack)]
        query = jnp.concatenate([query_ref[:, c] for c in columns], axis=0)
        scores = lax.dot_general(
            query, keys[...], (((1,), (1,)), ((), ())), preferred_element_type=jnp.float32
        )
        scores = jnp.where(allowed, scores * scaling, -jnp.inf)
        weights = jnp.exp(scores - jnp.max(scores, axis=1, keepdims=True))
        totals = jnp.sum(weights, axis=1, keepdims=True)
        result = jnp.dot(
            weights.astype(jnp.bfloat16), values[...], preferred_element_type=jnp.float32
        )
        result = (result / totals).astype(jnp.bfloat16)
        for h, c in enumerate(columns):
            out_ref[:, c] = result[h * rows : (h + 1) * rows]


def attend(queries, allowed, pieces):
    rows, width = queries.shape
    window = allowed.shape[1]
    group = QPK * HD
    stack = 4 if window <= 1024 else 1
    return pl.pallas_call(
        functools.partial(attend_kernel, len(pieces), QPK, stack),
        grid=(width // group,),
        in_specs=[
            pl.BlockSpec((rows, group), lambda i: (0, i)),
            pl.BlockSpec((rows, window), lambda i: (0, 0)),
        ]
        + [pl.BlockSpec((rows, 2 * HD), lambda i: (0, i))] * len(pieces),
        out_specs=pl.BlockSpec((rows, group), lambda i: (0, i)),
        out_shape=jax.ShapeDtypeStruct((rows, width), jnp.bfloat16),
        scratch_shapes=[pltpu.VMEM((window, HD), jnp.bfloat16)] * 2,
        compiler_params=pltpu.CompilerParams(vmem_limit_bytes=VMEM_LIMIT),
        name="attend",
    )(queries, allowed, *pieces)


def on_device(sizes, low, hidden, codes, scales, queries, segment_ids):
    groups, shards, cores = sizes
    rows = hidden.shape[0]
    features, width = codes.shape
    members = groups * low
    depth = features // members
    group = lax.axis_index("groups")
    lo = lax.axis_index("lo")
    shard = lax.axis_index("hi") * low + lo
    core = lax.axis_index("tensor")

    turns = turns_of(sizes, low, depth)
    place = (group, lo // 2, lo % 2, core, (shard * width) // BLK, group * low + lo)
    table = jnp.stack([jnp.asarray(p, jnp.int32) for p in place])

    ids = segment_ids.astype(jnp.bfloat16).reshape(rows // width, width)
    ids = jnp.pad(ids, ((0, PAD - rows // width), (0, 0)))
    weight = scaled_weight(turns, table, low, shards, codes, scales, ids)
    weight = lax.all_to_all(weight, SHARD, 0, 0, tiled=True)

    arrays, copies = spread_hidden(turns, place, sizes, low, hidden)
    other, mine = project(turns, arrays, copies, weight, table)
    swap = flat_pairs(sizes, lambda g, s, c: (g, s, 1 - c))
    partial = split(mine, lax.ppermute(other, ALL, swap))
    partial = lax.all_to_all(partial, BLOCK, 0, 0, tiled=True)
    total = jnp.sum(partial.astype(jnp.float32), axis=0)
    columns = mine.shape[2]
    rest = total[:, columns:].reshape(rows, -1, 1, HD)
    rest = jnp.concatenate([rest, jnp.zeros_like(rest)], axis=2).reshape(rows, columns)
    keyval = (total[:, :columns] + rest).astype(jnp.bfloat16)

    back = min(shards // 2 + 1, shards - 1)
    known = weight[:, depth : depth + rows // width, :].reshape(shards, rows)
    from_shard = shard - jnp.arange(back + 1, dtype=jnp.int32)
    seen = known[jnp.maximum(from_shard, 0)].reshape(-1)
    offset = jnp.arange(rows, dtype=jnp.int32)
    keypos = (from_shard[:, None] * rows + offset[None, :]).reshape(-1)
    rowpos = shard * rows + offset
    allowed = (
        (segment_ids.astype(jnp.bfloat16)[:, None] == seen[None, :])
        & (keypos[None, :] <= rowpos[:, None])
        & (keypos[None, :] >= 0)
    ).astype(jnp.float32)

    pieces = [keyval]
    for d in range(1, back + 1):
        up = flat_pairs(sizes, lambda g, s, c: (g, s + d, c) if s + d < shards else None)
        pieces.append(lax.ppermute(keyval, ALL, up))
    return attend(queries, allowed, pieces)


def solution(mesh):
    sizes = tuple(mesh.shape[name] for name in ("groups", "shard", "tensor"))
    groups, shards, cores = sizes
    low = math.gcd(shards, 4)
    fine = Mesh(mesh.devices.reshape(groups, shards // low, low, cores), ALL)
    tokens = ("groups", "hi", "lo")
    in_specs = (
        P(tokens, "tensor"),
        P("tensor", ("hi", "lo")),
        P("tensor", None),
        P(tokens, "tensor"),
        P(tokens),
    )
    return jax.shard_map(
        functools.partial(on_device, sizes, low),
        mesh=fine,
        in_specs=in_specs,
        out_specs=P(tokens, "tensor"),
        check_vma=False,
    )
```

```python
import functools
import math

import jax
import jax.numpy as jnp
from jax import lax
from jax.experimental import pallas as pl
from jax.experimental.pallas import tpu as pltpu
from jax.sharding import Mesh
from jax.sharding import PartitionSpec as P

KVH = 4
HD = 128
QPK = 16
BLK = 128
KVW = 1024
PAD = 16
SHARD = ("hi", "zz", "y")
ALL = ("groups",) + SHARD + ("tensor",)
BLOCK = ("groups", "zz")
MIB = 2**20


def after(value, *others):
    return lax.optimization_barrier((value,) + others)[0]


def flat_pairs(sizes, move):
    groups, shards, cores = sizes
    pairs = []
    for g in range(groups):
        for s in range(shards):
            for c in range(cores):
                to = move(g, s, c)
                if to is not None:
                    pairs.append(((g * shards + s) * cores + c, (to[0] * shards + to[1]) * cores + to[2]))
    return pairs


def scale_kernel(first_ref, codes_ref, scales_ref, ids_ref, near_ref, far_ref):
    depth = near_ref.shape[0] - PAD
    blocks = depth // BLK
    own, column, block = first_ref[0], first_ref[1], first_ref[2]
    for out_ref, which in ((near_ref, own), (far_ref, 1 - own)):
        for k in range(blocks):
            row = pl.multiple_of((which * blocks + k) * BLK, BLK)
            scale = scales_ref[column, block + which * blocks + k]
            part = codes_ref[pl.ds(row, BLK), :].astype(jnp.float32) * scale
            out_ref[k * BLK : (k + 1) * BLK, :] = part.astype(jnp.bfloat16)
        ids = ids_ref[...].astype(jnp.float32)
        out_ref[depth:, :] = jnp.broadcast_to(ids, (PAD, ids.shape[1])).astype(jnp.bfloat16)


def scaled_weight(codes, scales, segment_ids, depth, group, zz, column):
    width = codes.shape[1]
    share = 2 * depth
    first = jnp.stack([zz, column, group * (share // BLK), group]).astype(jnp.int32)
    out = jax.ShapeDtypeStruct((depth + PAD, width), jnp.bfloat16)
    whole = pl.BlockSpec((depth + PAD, width), lambda i, f: (0, 0))
    return pl.pallas_call(
        scale_kernel,
        grid_spec=pltpu.PrefetchScalarGridSpec(
            num_scalar_prefetch=1,
            grid=(1,),
            in_specs=[
                pl.BlockSpec((share, width), lambda i, f: (f[3], 0)),
                pl.BlockSpec(memory_space=pltpu.SMEM),
                pl.BlockSpec((1, width), lambda i, f: (0, 0)),
            ],
            out_specs=[whole, whole],
        ),
        out_shape=[out, out],
        compiler_params=pltpu.CompilerParams(vmem_limit_bytes=8 * MIB),
        name="scale",
    )(first, codes, scales.T, segment_ids.reshape(1, -1))


def gather_by_steps(sizes, hidden, codes, scales, segment_ids):
    rows, features = hidden.shape
    depth = features // 4
    group, zz, y = lax.axis_index("groups"), lax.axis_index("zz"), lax.axis_index("y")
    shard = (lax.axis_index("hi") * 2 + zz) * 2 + y
    member = group * 2 + zz

    def send(value, move):
        return lax.ppermute(value, ALL, flat_pairs(sizes, move))

    def along_shard(distance):
        return lambda g, s, c: (g, s ^ distance, c)

    near, far = scaled_weight(
        codes, scales, segment_ids, depth, group, zz, shard * codes.shape[1] // BLK
    )
    piece = {0: near}
    piece[6] = send(far, along_shard(6))
    piece[2] = send(far, along_shard(2))
    piece[1] = send(near, along_shard(1))
    sent = lax.dynamic_slice_in_dim(after(hidden, near), (1 - group) * 2 * depth, 2 * depth, 1)
    across = send(sent, lambda g, s, c: (1 - g, s, c))
    piece[4] = send(after(near, piece[2], piece[1]), along_shard(4))
    piece[3] = send(piece[2], along_shard(1))
    pair = jnp.concatenate(
        [
            lax.dynamic_slice_in_dim(hidden, (group * 2 + 1 - zz) * depth, depth, 1),
            lax.dynamic_slice_in_dim(across, (1 - zz) * depth, depth, 1),
        ],
        axis=0,
    )
    pair = send(pair, along_shard(2))
    piece[7] = send(after(piece[6], piece[3]), along_shard(1))
    piece[5] = send(after(piece[4], piece[7]), along_shard(1))
    order = sorted(piece)
    shards = jnp.stack([jnp.bitwise_xor(shard, d) for d in order]).astype(jnp.int32)
    arrays = [hidden, across, pair]
    copies = [
        (0, 0, member * depth, member),
        (1, 0, zz * depth, jnp.bitwise_xor(member, 2)),
        (2, 0, 0, jnp.bitwise_xor(member, 1)),
        (2, rows, 0, jnp.bitwise_xor(member, 3)),
    ]
    ids = [piece[d][depth : depth + 1] for d in order]
    known = jnp.concatenate(ids, axis=0)
    spot = jnp.bitwise_xor(shard, jnp.arange(8, dtype=jnp.int32))
    return arrays, copies, [piece[d] for d in order], shards, known[spot]


def gather_whole(sizes, hidden, codes, scales, segment_ids):
    groups = sizes[0]
    pair = lax.axis_size("zz")
    members = groups * pair
    rows, features = hidden.shape
    depth = features // members
    width = codes.shape[1]
    shards = sizes[1]
    shard = lax.axis_index(SHARD)
    share = pair * depth
    sliced = jnp.moveaxis(hidden.reshape(rows, members, depth), 1, 0)
    got = lax.all_to_all(sliced, BLOCK, 0, 0, tiled=True).reshape(members * rows, depth)
    copies = [(0, m * rows, 0, m) for m in range(members)]

    blocks = share // BLK
    group = lax.axis_index("groups")
    column = lax.dynamic_slice_in_dim(scales, (shard * width) // BLK, 1, 1)
    column = lax.dynamic_slice_in_dim(column, group * blocks, blocks, 0)
    held = lax.dynamic_slice_in_dim(codes, group * share, share, 0)
    weight = (held.astype(jnp.float32).reshape(blocks, BLK, width) * column[:, :, None]).astype(
        jnp.bfloat16
    )
    weight = weight.reshape(pair, depth, width)
    ids = segment_ids.astype(jnp.bfloat16).reshape(rows // width, width)
    ids = jnp.pad(ids, ((0, PAD - rows // width), (0, 0)))
    weight = jnp.concatenate([weight, jnp.broadcast_to(ids, (pair, PAD, width))], axis=1)
    high = lax.axis_size("hi")
    weight = jnp.broadcast_to(weight[None], (high,) + weight.shape)
    weight = weight.reshape(high * pair, depth + PAD, width)
    weight = lax.all_to_all(weight, ("hi", "zz"), 0, 0, tiled=True)
    weight = lax.all_gather(weight, "y", axis=1).reshape(shards, depth + PAD, width)
    known = weight[:, depth : depth + rows // width, :].reshape(shards, rows)
    weight = jnp.moveaxis(weight[:, :depth].reshape(2, shards // 2, depth, width), 1, 2)
    halves = weight.reshape(2, depth, shards * width // 2)
    return [got], copies, [halves[0], halves[1]], jnp.arange(2, dtype=jnp.int32), known


def project_kernel(copies, sources, columns, rows_ref, first_ref, member_ref, shard_ref, core_ref, *refs):
    hidden_refs, refs = refs[:sources], refs[sources:]
    weight_refs, (other_ref, mine_ref, left, halves, sems) = refs[:-5], refs[-5:]
    step = pl.program_id(0)
    rows = mine_ref.shape[1]
    depth = left.shape[1]
    core = core_ref[0]

    @pl.when(step == 0)
    def _():
        started = []
        for k, at in enumerate(copies):
            first = pl.multiple_of(first_ref[k], 128)
            row = pl.multiple_of(rows_ref[k], 16)
            to = pl.multiple_of(member_ref[k] * rows, rows)
            started.append(
                pltpu.make_async_copy(
                    hidden_refs[at].at[pl.ds(row, rows), pl.ds(first, depth)],
                    left.at[pl.ds(to, rows), :],
                    sems.at[k],
                )
            )
        for k, ref in enumerate(weight_refs):
            width = ref.shape[1]
            first = shard_ref[k] * width
            half = jnp.bitwise_xor(core, first // columns)
            at = pl.multiple_of(first % columns, 128)
            started.append(
                pltpu.make_async_copy(
                    ref.at[pl.ds(0, depth), :],
                    halves.at[half, :, pl.ds(at, width)],
                    sems.at[len(copies) + k],
                )
            )
        for copy in started:
            copy.start()
        for copy in started:
            copy.wait()

    size = mine_ref.shape[2]
    per_half = columns // size
    for half, out_ref in ((1, other_ref), (0, mine_ref)):
        for k in range(per_half):

            @pl.when(step == (1 - half) * per_half + k)
            def _():
                total = jnp.dot(
                    left[...],
                    halves[half, :, k * size : (k + 1) * size],
                    preferred_element_type=jnp.float32,
                )
                out_ref[...] = total.reshape(out_ref.shape)


def project(arrays, copies, pieces, shards, core, rows):
    members = len(copies)
    width = pieces[0].shape[1]
    columns = len(pieces) * width // 2
    depth = arrays[-1].shape[1]
    table = [jnp.stack([jnp.asarray(c[i], jnp.int32) for c in copies]) for i in (1, 2, 3)]
    size = 256
    per_half = columns // size
    out = jax.ShapeDtypeStruct((members, rows, columns), jnp.float32)
    return pl.pallas_call(
        functools.partial(project_kernel, [c[0] for c in copies], len(arrays), columns),
        grid_spec=pltpu.PrefetchScalarGridSpec(
            num_scalar_prefetch=5,
            grid=(2 * per_half,),
            in_specs=[pl.BlockSpec(memory_space=pl.ANY)] * (len(arrays) + len(pieces)),
            out_specs=[
                pl.BlockSpec((members, rows, size), lambda i, *_: (0, 0, jnp.minimum(i, per_half - 1))),
                pl.BlockSpec((members, rows, size), lambda i, *_: (0, 0, jnp.maximum(i - per_half, 0))),
            ],
            scratch_shapes=[
                pltpu.VMEM((members * rows, depth), jnp.bfloat16),
                pltpu.VMEM((2, depth, columns), jnp.bfloat16),
                pltpu.SemaphoreType.DMA((len(copies) + len(pieces),)),
            ],
        ),
        out_shape=[out, out],
        compiler_params=pltpu.CompilerParams(vmem_limit_bytes=24 * MIB),
        name="project",
    )(*table, shards, core, *arrays, *pieces)


def split_kernel(mine_ref, got_ref, out_ref):
    total = mine_ref[...] + got_ref[...]
    columns = total.shape[2]
    out_ref[:, :, :columns] = total.astype(jnp.bfloat16)
    for head in range(columns // (2 * HD)):
        keys = total[:, :, 2 * head * HD : (2 * head + 1) * HD]
        rest = keys - keys.astype(jnp.bfloat16).astype(jnp.float32)
        at = columns + head * HD
        out_ref[:, :, at : at + HD] = rest.astype(jnp.bfloat16)


def split(mine, got):
    members, rows, columns = mine.shape
    spec = pl.BlockSpec((1, rows, columns), lambda i: (i, 0, 0))
    wide = columns + columns // 2
    return pl.pallas_call(
        split_kernel,
        grid=(members,),
        in_specs=[spec, spec],
        out_specs=pl.BlockSpec((1, rows, wide), lambda i: (i, 0, 0)),
        out_shape=jax.ShapeDtypeStruct((members, rows, wide), jnp.bfloat16),
        compiler_params=pltpu.CompilerParams(vmem_limit_bytes=24 * MIB),
        name="split",
    )(mine, got)


def attend_kernel(pieces, heads, stack, query_ref, allowed_ref, *refs):
    kv_refs, (out_ref, keys, values) = refs[:pieces], refs[pieces:]
    rows = query_ref.shape[0]
    scaling = 1.0 / math.sqrt(HD)
    for d, ref in enumerate(kv_refs):
        keys[d * rows : (d + 1) * rows, :] = ref[:, :HD]
        values[d * rows : (d + 1) * rows, :] = ref[:, HD:]
    allowed = allowed_ref[...]
    allowed = jnp.concatenate([allowed] * stack, axis=0) > 0.0
    for part in range(heads // stack):
        columns = [slice((part * stack + h) * HD, (part * stack + h + 1) * HD) for h in range(stack)]
        query = jnp.concatenate([query_ref[:, c] for c in columns], axis=0)
        scores = lax.dot_general(
            query, keys[...], (((1,), (1,)), ((), ())), preferred_element_type=jnp.float32
        )
        scores = jnp.where(allowed, scores * scaling, -jnp.inf)
        weights = jnp.exp(scores - jnp.max(scores, axis=1, keepdims=True))
        totals = jnp.sum(weights, axis=1, keepdims=True)
        result = jnp.dot(
            weights.astype(jnp.bfloat16), values[...], preferred_element_type=jnp.float32
        )
        result = (result / totals).astype(jnp.bfloat16)
        for h, c in enumerate(columns):
            out_ref[:, c] = result[h * rows : (h + 1) * rows]


def attend(queries, allowed, pieces):
    rows, width = queries.shape
    window = allowed.shape[1]
    group = QPK * HD
    stack = 4 if window <= 1024 else 1
    return pl.pallas_call(
        functools.partial(attend_kernel, len(pieces), QPK, stack),
        grid=(width // group,),
        in_specs=[
            pl.BlockSpec((rows, group), lambda i: (0, i)),
            pl.BlockSpec((rows, window), lambda i: (0, 0)),
        ]
        + [pl.BlockSpec((rows, 2 * HD), lambda i: (0, i))] * len(pieces),
        out_specs=pl.BlockSpec((rows, group), lambda i: (0, i)),
        out_shape=jax.ShapeDtypeStruct((rows, width), jnp.bfloat16),
        scratch_shapes=[pltpu.VMEM((window, HD), jnp.bfloat16)] * 2,
        compiler_params=pltpu.CompilerParams(vmem_limit_bytes=24 * MIB),
        name="attend",
    )(queries, allowed, *pieces)


def on_device(sizes, hidden, codes, scales, queries, segment_ids):
    groups, shards, cores = sizes
    rows = hidden.shape[0]
    shard = lax.axis_index(SHARD)
    core = lax.axis_index("tensor").astype(jnp.int32)
    by_steps = groups == 2 and shards == 8 and codes.shape[1] == BLK and rows == BLK
    gather = gather_by_steps if by_steps else gather_whole
    arrays, copies, pieces, where, known = gather(sizes, hidden, codes, scales, segment_ids)
    other, mine = project(arrays, copies, pieces, where, core[None], rows)
    swap = flat_pairs(sizes, lambda g, s, c: (g, s, 1 - c))
    partial = split(mine, lax.ppermute(other, ALL, swap))
    partial = lax.all_to_all(partial, BLOCK, 0, 0, tiled=True)
    total = jnp.sum(partial.astype(jnp.float32), axis=0)
    columns = mine.shape[2]
    rest = total[:, columns:].reshape(rows, -1, 1, HD)
    rest = jnp.concatenate([rest, jnp.zeros_like(rest)], axis=2).reshape(rows, columns)
    keyval = (total[:, :columns] + rest).astype(jnp.bfloat16)

    back = min(shards // 2 + 1, shards - 1)
    from_shard = shard - jnp.arange(back + 1, dtype=jnp.int32)
    seen = known[jnp.maximum(from_shard, 0)].reshape(-1)
    offset = jnp.arange(rows, dtype=jnp.int32)
    keypos = (from_shard[:, None] * rows + offset[None, :]).reshape(-1)
    rowpos = shard * rows + offset
    allowed = (
        (segment_ids.astype(jnp.bfloat16)[:, None] == seen[None, :])
        & (keypos[None, :] <= rowpos[:, None])
        & (keypos[None, :] >= 0)
    ).astype(jnp.float32)

    pieces = [keyval]
    for d in range(1, back + 1):
        up = flat_pairs(sizes, lambda g, s, c: (g, s + d, c) if s + d < shards else None)
        pieces.append(lax.ppermute(keyval, ALL, up))
    return attend(queries, allowed, pieces)


def solution(mesh):
    sizes = tuple(mesh.shape[name] for name in ("groups", "shard", "tensor"))
    groups, shards, cores = sizes
    y = math.gcd(shards, 2)
    zz = math.gcd(shards // y, 2)
    fine = Mesh(mesh.devices.reshape(groups, shards // (y * zz), zz, y, cores), ALL)
    tokens = ("groups",) + SHARD
    in_specs = (
        P(tokens, "tensor"),
        P("tensor", SHARD),
        P("tensor", None),
        P(tokens, "tensor"),
        P(tokens),
    )
    return jax.shard_map(
        functools.partial(on_device, sizes),
        mesh=fine,
        in_specs=in_specs,
        out_specs=P(tokens, "tensor"),
        check_vma=False,
    )
```

```python
import functools
import math

import jax
import jax.numpy as jnp
from jax import lax
from jax.experimental import pallas as pl
from jax.experimental.pallas import tpu as pltpu
from jax.sharding import Mesh
from jax.sharding import PartitionSpec as P

KVH = 4
HD = 128
QPK = 16
BLK = 128
KVW = 1024
PAD = 16
SHARD = ("hi", "zz", "y")
ALL = ("groups",) + SHARD + ("tensor",)
BLOCK = ("groups", "zz")
MIB = 2**20


def after(value, *others):
    return lax.optimization_barrier((value,) + others)[0]


def flat_pairs(sizes, move):
    groups, shards, cores = sizes
    pairs = []
    for g in range(groups):
        for s in range(shards):
            for c in range(cores):
                to = move(g, s, c)
                if to is not None:
                    pairs.append(((g * shards + s) * cores + c, (to[0] * shards + to[1]) * cores + to[2]))
    return pairs


def scale_kernel(first_ref, codes_ref, scales_ref, ids_ref, near_ref, far_ref, held, sems):
    depth = near_ref.shape[0] - PAD
    blocks = depth // BLK
    own, column, block = first_ref[0], first_ref[1], first_ref[2]
    copies = []
    for k, which in enumerate((1 - own, own)):
        row = pl.multiple_of((block + which * blocks) * BLK, BLK)
        copies.append(
            pltpu.make_async_copy(codes_ref.at[pl.ds(row, depth), :], held.at[k], sems.at[k])
        )
        copies[k].start()
    ids = ids_ref[...].astype(jnp.float32)
    ids = jnp.broadcast_to(ids, (PAD, ids.shape[1])).astype(jnp.bfloat16)
    for k, (out_ref, which) in enumerate(((far_ref, 1 - own), (near_ref, own))):
        copies[k].wait()
        for b in range(blocks):
            scale = scales_ref[column, block + which * blocks + b]
            part = held[k, b * BLK : (b + 1) * BLK, :].astype(jnp.float32) * scale
            out_ref[b * BLK : (b + 1) * BLK, :] = part.astype(jnp.bfloat16)
        out_ref[depth:, :] = ids


def scaled_weight(codes, scales, segment_ids, depth, group, zz, column):
    width = codes.shape[1]
    first = jnp.stack([zz, column, group * (2 * depth // BLK)]).astype(jnp.int32)
    out = jax.ShapeDtypeStruct((depth + PAD, width), jnp.bfloat16)
    return pl.pallas_call(
        scale_kernel,
        in_specs=[
            pl.BlockSpec(memory_space=pltpu.SMEM),
            pl.BlockSpec(memory_space=pltpu.HBM),
            pl.BlockSpec(memory_space=pltpu.SMEM),
            pl.BlockSpec(memory_space=pltpu.VMEM),
        ],
        out_specs=[pl.BlockSpec(memory_space=pltpu.VMEM)] * 2,
        out_shape=[out, out],
        scratch_shapes=[
            pltpu.VMEM((2, depth, width), jnp.bfloat16),
            pltpu.SemaphoreType.DMA((2,)),
        ],
        compiler_params=pltpu.CompilerParams(vmem_limit_bytes=8 * MIB),
        name="scale",
    )(first, codes, scales.T, segment_ids.reshape(1, -1))


def gather_by_steps(sizes, hidden, codes, scales, segment_ids):
    rows, features = hidden.shape
    depth = features // 4
    group, zz, y = lax.axis_index("groups"), lax.axis_index("zz"), lax.axis_index("y")
    shard = (lax.axis_index("hi") * 2 + zz) * 2 + y
    member = group * 2 + zz

    def send(value, move):
        return lax.ppermute(value, ALL, flat_pairs(sizes, move))

    def along_shard(distance):
        return lambda g, s, c: (g, s ^ distance, c)

    sent = lax.dynamic_slice_in_dim(hidden, (1 - group) * 2 * depth, 2 * depth, 1)
    across = send(sent, lambda g, s, c: (1 - g, s, c))
    near, far = scaled_weight(
        after(codes, sent), scales, segment_ids, depth, group, zz, shard * codes.shape[1] // BLK
    )
    piece = {0: near}
    piece[6] = send(far, along_shard(6))
    piece[2] = send(far, along_shard(2))
    piece[1] = send(near, along_shard(1))
    pair = jnp.concatenate(
        [
            lax.dynamic_slice_in_dim(hidden, (group * 2 + 1 - zz) * depth, depth, 1),
            lax.dynamic_slice_in_dim(across, (1 - zz) * depth, depth, 1),
        ],
        axis=0,
    )
    piece[4] = send(after(near, pair, piece[2], piece[1]), along_shard(4))
    pair = send(pair, along_shard(2))
    piece[3] = send(piece[2], along_shard(1))
    piece[7] = send(after(piece[6], piece[3]), along_shard(1))
    piece[5] = send(after(piece[4], piece[7]), along_shard(1))
    order = sorted(piece)
    shards = jnp.stack([jnp.bitwise_xor(shard, d) for d in order]).astype(jnp.int32)
    arrays = [hidden, across, pair]
    copies = [
        (0, 0, member * depth, member),
        (1, 0, zz * depth, jnp.bitwise_xor(member, 2)),
        (2, 0, 0, jnp.bitwise_xor(member, 1)),
        (2, rows, 0, jnp.bitwise_xor(member, 3)),
    ]
    ids = [piece[d][depth : depth + 1] for d in order]
    known = jnp.concatenate(ids, axis=0)
    spot = jnp.bitwise_xor(shard, jnp.arange(8, dtype=jnp.int32))
    return arrays, copies, [piece[d] for d in order], shards, known[spot]


def gather_whole(sizes, hidden, codes, scales, segment_ids):
    groups = sizes[0]
    pair = lax.axis_size("zz")
    members = groups * pair
    rows, features = hidden.shape
    depth = features // members
    width = codes.shape[1]
    shards = sizes[1]
    shard = lax.axis_index(SHARD)
    share = pair * depth
    sliced = jnp.moveaxis(hidden.reshape(rows, members, depth), 1, 0)
    got = lax.all_to_all(sliced, BLOCK, 0, 0, tiled=True).reshape(members * rows, depth)
    copies = [(0, m * rows, 0, m) for m in range(members)]

    blocks = share // BLK
    group = lax.axis_index("groups")
    column = lax.dynamic_slice_in_dim(scales, (shard * width) // BLK, 1, 1)
    column = lax.dynamic_slice_in_dim(column, group * blocks, blocks, 0)
    held = lax.dynamic_slice_in_dim(codes, group * share, share, 0)
    weight = (held.astype(jnp.float32).reshape(blocks, BLK, width) * column[:, :, None]).astype(
        jnp.bfloat16
    )
    weight = weight.reshape(pair, depth, width)
    ids = segment_ids.astype(jnp.bfloat16).reshape(rows // width, width)
    ids = jnp.pad(ids, ((0, PAD - rows // width), (0, 0)))
    weight = jnp.concatenate([weight, jnp.broadcast_to(ids, (pair, PAD, width))], axis=1)
    high = lax.axis_size("hi")
    weight = jnp.broadcast_to(weight[None], (high,) + weight.shape)
    weight = weight.reshape(high * pair, depth + PAD, width)
    weight = lax.all_to_all(weight, ("hi", "zz"), 0, 0, tiled=True)
    weight = lax.all_gather(weight, "y", axis=1).reshape(shards, depth + PAD, width)
    known = weight[:, depth : depth + rows // width, :].reshape(shards, rows)
    weight = jnp.moveaxis(weight[:, :depth].reshape(2, shards // 2, depth, width), 1, 2)
    halves = weight.reshape(2, depth, shards * width // 2)
    return [got], copies, [halves[0], halves[1]], jnp.arange(2, dtype=jnp.int32), known


def project_kernel(copies, sources, columns, rows_ref, first_ref, member_ref, shard_ref, core_ref, *refs):
    hidden_refs, refs = refs[:sources], refs[sources:]
    weight_refs, (other_ref, mine_ref, left, halves, sems) = refs[:-5], refs[-5:]
    step = pl.program_id(0)
    rows = mine_ref.shape[1]
    depth = left.shape[1]
    core = core_ref[0]

    @pl.when(step == 0)
    def _():
        started = []
        for k, at in enumerate(copies):
            first = pl.multiple_of(first_ref[k], 128)
            row = pl.multiple_of(rows_ref[k], 16)
            to = pl.multiple_of(member_ref[k] * rows, rows)
            started.append(
                pltpu.make_async_copy(
                    hidden_refs[at].at[pl.ds(row, rows), pl.ds(first, depth)],
                    left.at[pl.ds(to, rows), :],
                    sems.at[k],
                )
            )
        for k, ref in enumerate(weight_refs):
            width = ref.shape[1]
            first = shard_ref[k] * width
            half = jnp.bitwise_xor(core, first // columns)
            at = pl.multiple_of(first % columns, 128)
            started.append(
                pltpu.make_async_copy(
                    ref.at[pl.ds(0, depth), :],
                    halves.at[half, :, pl.ds(at, width)],
                    sems.at[len(copies) + k],
                )
            )
        for copy in started:
            copy.start()
        for copy in started:
            copy.wait()

    size = mine_ref.shape[2]
    per_half = columns // size
    for half, out_ref in ((1, other_ref), (0, mine_ref)):
        for k in range(per_half):

            @pl.when(step == (1 - half) * per_half + k)
            def _():
                total = jnp.dot(
                    left[...],
                    halves[half, :, k * size : (k + 1) * size],
                    preferred_element_type=jnp.float32,
                )
                out_ref[...] = total.reshape(out_ref.shape)


def project(arrays, copies, pieces, shards, core, rows):
    members = len(copies)
    width = pieces[0].shape[1]
    columns = len(pieces) * width // 2
    depth = arrays[-1].shape[1]
    table = [jnp.stack([jnp.asarray(c[i], jnp.int32) for c in copies]) for i in (1, 2, 3)]
    size = 256
    per_half = columns // size
    out = jax.ShapeDtypeStruct((members, rows, columns), jnp.float32)
    return pl.pallas_call(
        functools.partial(project_kernel, [c[0] for c in copies], len(arrays), columns),
        grid_spec=pltpu.PrefetchScalarGridSpec(
            num_scalar_prefetch=5,
            grid=(2 * per_half,),
            in_specs=[pl.BlockSpec(memory_space=pl.ANY)] * (len(arrays) + len(pieces)),
            out_specs=[
                pl.BlockSpec((members, rows, size), lambda i, *_: (0, 0, jnp.minimum(i, per_half - 1))),
                pl.BlockSpec((members, rows, size), lambda i, *_: (0, 0, jnp.maximum(i - per_half, 0))),
            ],
            scratch_shapes=[
                pltpu.VMEM((members * rows, depth), jnp.bfloat16),
                pltpu.VMEM((2, depth, columns), jnp.bfloat16),
                pltpu.SemaphoreType.DMA((len(copies) + len(pieces),)),
            ],
        ),
        out_shape=[out, out],
        compiler_params=pltpu.CompilerParams(vmem_limit_bytes=24 * MIB),
        name="project",
    )(*table, shards, core, *arrays, *pieces)


def split_kernel(mine_ref, got_ref, out_ref):
    total = mine_ref[...] + got_ref[...]
    columns = total.shape[2]
    out_ref[:, :, :columns] = total.astype(jnp.bfloat16)
    for head in range(columns // (2 * HD)):
        keys = total[:, :, 2 * head * HD : (2 * head + 1) * HD]
        rest = keys - keys.astype(jnp.bfloat16).astype(jnp.float32)
        at = columns + head * HD
        out_ref[:, :, at : at + HD] = rest.astype(jnp.bfloat16)


def split(mine, got):
    members, rows, columns = mine.shape
    spec = pl.BlockSpec((1, rows, columns), lambda i: (i, 0, 0))
    wide = columns + columns // 2
    return pl.pallas_call(
        split_kernel,
        grid=(members,),
        in_specs=[spec, spec],
        out_specs=pl.BlockSpec((1, rows, wide), lambda i: (i, 0, 0)),
        out_shape=jax.ShapeDtypeStruct((members, rows, wide), jnp.bfloat16),
        compiler_params=pltpu.CompilerParams(vmem_limit_bytes=24 * MIB),
        name="split",
    )(mine, got)


def attend_kernel(pieces, heads, stack, query_ref, allowed_ref, *refs):
    kv_refs, (out_ref, keys, values) = refs[:pieces], refs[pieces:]
    rows = query_ref.shape[0]
    scaling = 1.0 / math.sqrt(HD)
    for d, ref in enumerate(kv_refs):
        keys[d * rows : (d + 1) * rows, :] = ref[:, :HD]
        values[d * rows : (d + 1) * rows, :] = ref[:, HD:]
    allowed = allowed_ref[...]
    allowed = jnp.concatenate([allowed] * stack, axis=0) > 0.0
    for part in range(heads // stack):
        columns = [slice((part * stack + h) * HD, (part * stack + h + 1) * HD) for h in range(stack)]
        query = jnp.concatenate([query_ref[:, c] for c in columns], axis=0)
        scores = lax.dot_general(
            query, keys[...], (((1,), (1,)), ((), ())), preferred_element_type=jnp.float32
        )
        scores = jnp.where(allowed, scores * scaling, -jnp.inf)
        weights = jnp.exp(scores - jnp.max(scores, axis=1, keepdims=True))
        totals = jnp.sum(weights, axis=1, keepdims=True)
        result = jnp.dot(
            weights.astype(jnp.bfloat16), values[...], preferred_element_type=jnp.float32
        )
        result = (result / totals).astype(jnp.bfloat16)
        for h, c in enumerate(columns):
            out_ref[:, c] = result[h * rows : (h + 1) * rows]


def attend(queries, allowed, pieces):
    rows, width = queries.shape
    window = allowed.shape[1]
    group = QPK * HD
    stack = 4 if window <= 1024 else 1
    return pl.pallas_call(
        functools.partial(attend_kernel, len(pieces), QPK, stack),
        grid=(width // group,),
        in_specs=[
            pl.BlockSpec((rows, group), lambda i: (0, i)),
            pl.BlockSpec((rows, window), lambda i: (0, 0)),
        ]
        + [pl.BlockSpec((rows, 2 * HD), lambda i: (0, i))] * len(pieces),
        out_specs=pl.BlockSpec((rows, group), lambda i: (0, i)),
        out_shape=jax.ShapeDtypeStruct((rows, width), jnp.bfloat16),
        scratch_shapes=[pltpu.VMEM((window, HD), jnp.bfloat16)] * 2,
        compiler_params=pltpu.CompilerParams(vmem_limit_bytes=24 * MIB),
        name="attend",
    )(queries, allowed, *pieces)


def on_device(sizes, hidden, codes, scales, queries, segment_ids):
    groups, shards, cores = sizes
    rows = hidden.shape[0]
    shard = lax.axis_index(SHARD)
    core = lax.axis_index("tensor").astype(jnp.int32)
    by_steps = groups == 2 and shards == 8 and codes.shape[1] == BLK and rows == BLK
    gather = gather_by_steps if by_steps else gather_whole
    arrays, copies, pieces, where, known = gather(sizes, hidden, codes, scales, segment_ids)
    other, mine = project(arrays, copies, pieces, where, core[None], rows)
    swap = flat_pairs(sizes, lambda g, s, c: (g, s, 1 - c))
    partial = split(mine, lax.ppermute(other, ALL, swap))
    partial = lax.all_to_all(partial, BLOCK, 0, 0, tiled=True)
    total = jnp.sum(partial.astype(jnp.float32), axis=0)
    columns = mine.shape[2]
    rest = total[:, columns:].reshape(rows, -1, 1, HD)
    rest = jnp.concatenate([rest, jnp.zeros_like(rest)], axis=2).reshape(rows, columns)
    keyval = (total[:, :columns] + rest).astype(jnp.bfloat16)

    back = min(shards // 2 + 1, shards - 1)
    from_shard = shard - jnp.arange(back + 1, dtype=jnp.int32)
    seen = known[jnp.maximum(from_shard, 0)].reshape(-1)
    offset = jnp.arange(rows, dtype=jnp.int32)
    keypos = (from_shard[:, None] * rows + offset[None, :]).reshape(-1)
    rowpos = shard * rows + offset
    allowed = (
        (segment_ids.astype(jnp.bfloat16)[:, None] == seen[None, :])
        & (keypos[None, :] <= rowpos[:, None])
        & (keypos[None, :] >= 0)
    ).astype(jnp.float32)

    pieces = [keyval]
    for d in range(1, back + 1):
        up = flat_pairs(sizes, lambda g, s, c: (g, s + d, c) if s + d < shards else None)
        pieces.append(lax.ppermute(keyval, ALL, up))
    return attend(queries, allowed, pieces)


def solution(mesh):
    sizes = tuple(mesh.shape[name] for name in ("groups", "shard", "tensor"))
    groups, shards, cores = sizes
    y = math.gcd(shards, 2)
    zz = math.gcd(shards // y, 2)
    fine = Mesh(mesh.devices.reshape(groups, shards // (y * zz), zz, y, cores), ALL)
    tokens = ("groups",) + SHARD
    in_specs = (
        P(tokens, "tensor"),
        P("tensor", SHARD),
        P("tensor", None),
        P(tokens, "tensor"),
        P(tokens),
    )
    return jax.shard_map(
        functools.partial(on_device, sizes),
        mesh=fine,
        in_specs=in_specs,
        out_specs=P(tokens, "tensor"),
        check_vma=False,
    )
```

```python
import functools
import math

import jax
import jax.numpy as jnp
from jax import lax
from jax.experimental import pallas as pl
from jax.experimental.pallas import tpu as pltpu
from jax.sharding import Mesh
from jax.sharding import PartitionSpec as P

KVH = 4
HD = 128
QPK = 16
BLK = 128
KVW = 1024
PAD = 16
SHARD = ("hi", "zz", "y")
ALL = ("groups",) + SHARD + ("tensor",)
BLOCK = ("groups", "zz")
MIB = 2**20


def gate_kernel(value_ref, *refs):
    pass


def gate(value, *others):
    hbm = pl.BlockSpec(memory_space=pl.ANY)
    return pl.pallas_call(
        gate_kernel,
        in_specs=[hbm] * (1 + len(others)),
        out_specs=hbm,
        out_shape=jax.ShapeDtypeStruct(value.shape, value.dtype),
        input_output_aliases={0: 0},
        name="gate",
    )(value, *others)


def flat_pairs(sizes, move):
    groups, shards, cores = sizes
    pairs = []
    for g in range(groups):
        for s in range(shards):
            for c in range(cores):
                to = move(g, s, c)
                if to is not None:
                    pairs.append(((g * shards + s) * cores + c, (to[0] * shards + to[1]) * cores + to[2]))
    return pairs


def scale_kernel(first_ref, codes_ref, scales_ref, ids_ref, near_ref, far_ref, copy_ref, held, sems):
    depth = near_ref.shape[0] - PAD
    blocks = depth // BLK
    own, column, block = first_ref[0], first_ref[1], first_ref[2]
    copies = []
    for k, which in enumerate((1 - own, own)):
        row = pl.multiple_of((block + which * blocks) * BLK, BLK)
        copies.append(
            pltpu.make_async_copy(codes_ref.at[pl.ds(row, depth), :], held.at[k], sems.at[k])
        )
        copies[k].start()
    ids = ids_ref[...].astype(jnp.float32)
    ids = jnp.broadcast_to(ids, (PAD, ids.shape[1])).astype(jnp.bfloat16)
    for k, (out_ref, which) in enumerate(((far_ref, 1 - own), (near_ref, own))):
        copies[k].wait()
        for b in range(blocks):
            scale = scales_ref[column, block + which * blocks + b]
            part = held[k, b * BLK : (b + 1) * BLK, :].astype(jnp.float32) * scale
            out_ref[b * BLK : (b + 1) * BLK, :] = part.astype(jnp.bfloat16)
        out_ref[depth:, :] = ids
    copy_ref[...] = near_ref[...]


def scaled_weight(codes, scales, segment_ids, depth, group, zz, column):
    width = codes.shape[1]
    first = jnp.stack([zz, column, group * (2 * depth // BLK)]).astype(jnp.int32)
    out = jax.ShapeDtypeStruct((depth + PAD, width), jnp.bfloat16)
    return pl.pallas_call(
        scale_kernel,
        in_specs=[
            pl.BlockSpec(memory_space=pltpu.SMEM),
            pl.BlockSpec(memory_space=pltpu.HBM),
            pl.BlockSpec(memory_space=pltpu.SMEM),
            pl.BlockSpec(memory_space=pltpu.VMEM),
        ],
        out_specs=[pl.BlockSpec(memory_space=pltpu.VMEM)] * 3,
        out_shape=[out, out, out],
        scratch_shapes=[
            pltpu.VMEM((2, depth, width), jnp.bfloat16),
            pltpu.SemaphoreType.DMA((2,)),
        ],
        compiler_params=pltpu.CompilerParams(vmem_limit_bytes=56 * MIB),
        name="scale",
    )(first, codes, scales.T, segment_ids.reshape(1, -1))


def gather_by_steps(sizes, hidden, codes, scales, segment_ids):
    rows, features = hidden.shape
    depth = features // 4
    group, zz, y = lax.axis_index("groups"), lax.axis_index("zz"), lax.axis_index("y")
    shard = (lax.axis_index("hi") * 2 + zz) * 2 + y
    member = group * 2 + zz

    def send(value, move):
        return lax.ppermute(value, ALL, flat_pairs(sizes, move))

    def along_shard(distance):
        return lambda g, s, c: (g, s ^ distance, c)

    near, far, later = scaled_weight(
        codes, scales, segment_ids, depth, group, zz, shard * codes.shape[1] // BLK
    )
    sent = lax.dynamic_slice_in_dim(hidden, (1 - group) * 2 * depth, 2 * depth, 1)
    across = send(sent, lambda g, s, c: (1 - g, s, c))
    piece = {0: near}
    piece[6] = send(far, along_shard(6))
    piece[2] = send(far, along_shard(2))
    piece[1] = send(near, along_shard(1))
    piece[4] = send(gate(later, piece[2]), along_shard(4))
    pair = jnp.concatenate(
        [
            lax.dynamic_slice_in_dim(hidden, (group * 2 + 1 - zz) * depth, depth, 1),
            lax.dynamic_slice_in_dim(across, (1 - zz) * depth, depth, 1),
        ],
        axis=0,
    )
    pair = send(pair, along_shard(2))
    piece[3] = send(piece[2], along_shard(1))
    piece[6] = gate(piece[6], piece[3])
    piece[7] = send(piece[6], along_shard(1))
    piece[5] = send(piece[4], along_shard(1))
    arrays = [hidden, across, pair]
    copies = [(0, 0, member * depth), (2, 0, 0), (1, 0, zz * depth), (2, rows, 0)]
    return arrays, copies, piece


def head_kernel(copies, heads, early, table_ref, *refs):
    hidden_refs, refs = refs[:3], refs[3:]
    weight_refs, refs = refs[: 2 * heads], refs[2 * heads :]
    if early:
        mine_ref, other_ref, own_ref, ids_ref, left, right, sems = refs
    else:
        own_ref, mine_ref, other_ref, ids_ref, left, right, sems = refs
    rows, depth = mine_ref.shape[1], left.shape[1]
    count = len(copies)
    started = []
    for k, (at, row) in enumerate(copies):
        first = pl.multiple_of(table_ref[k], HD)
        started.append(
            pltpu.make_async_copy(
                hidden_refs[at].at[row : row + rows, pl.ds(first, depth)],
                left.at[k * rows : (k + 1) * rows, :],
                sems.at[k],
            )
        )
    for k, ref in enumerate(weight_refs):
        first = pl.multiple_of(jnp.bitwise_xor(table_ref[count], k % 2) * HD, HD)
        started.append(
            pltpu.make_async_copy(
                ref.at[pl.ds(0, depth), :], right.at[k // 2, :, pl.ds(first, HD)], sems.at[count + k]
            )
        )
    for k, ref in enumerate(weight_refs):
        started.append(
            pltpu.make_async_copy(
                ref.at[pl.ds(depth, PAD), :], ids_ref.at[k], sems.at[count + 2 * heads + k]
            )
        )
    for copy in started:
        copy.start()
    for copy in started[:count]:
        copy.wait()

    def head(h):
        for copy in started[count + 2 * h : count + 2 * h + 2]:
            copy.wait()
        total = jnp.dot(left[...], right[h], preferred_element_type=jnp.float32)
        return total.reshape(mine_ref.shape)

    def put(here, there, first, second):
        @pl.when(table_ref[count + 1] == 1)
        def _():
            here[...] = first
            if second is not None:
                there[...] = second

        @pl.when(table_ref[count + 1] == 0)
        def _():
            there[...] = first
            if second is not None:
                here[...] = second

    if early:
        put(mine_ref, other_ref, head(0), None)
        put(other_ref, mine_ref, head(1), None)
        own_ref[...] = head(2)
    else:
        put(mine_ref, other_ref, own_ref[...], head(0))
    for copy in started[count + 2 * heads :]:
        copy.wait()


def project_heads(early, arrays, copies, pieces, table, rows, own=None):
    heads = len(pieces) // 2
    depth = arrays[-1].shape[1]
    members = len(copies)
    out = jax.ShapeDtypeStruct((members, rows, 2 * HD), jnp.float32)
    ids = jax.ShapeDtypeStruct((len(pieces), PAD, HD), jnp.bfloat16)
    vmem = pl.BlockSpec(memory_space=pltpu.VMEM)
    extra = [] if early else [own]
    results = [out] * (3 if early else 2) + [ids]
    return pl.pallas_call(
        functools.partial(head_kernel, [c[:2] for c in copies], heads, early),
        in_specs=[pl.BlockSpec(memory_space=pltpu.SMEM)]
        + [pl.BlockSpec(memory_space=pl.ANY)] * (len(arrays) + len(pieces))
        + [vmem] * len(extra),
        out_specs=[vmem] * len(results),
        out_shape=results,
        scratch_shapes=[
            pltpu.VMEM((members * rows, depth), jnp.bfloat16),
            pltpu.VMEM((heads, depth, 2 * HD), jnp.bfloat16),
            pltpu.SemaphoreType.DMA((members + 2 * len(pieces),)),
        ],
        compiler_params=pltpu.CompilerParams(vmem_limit_bytes=24 * MIB),
        cost_estimate=pl.CostEstimate(
            flops=0 if early else 4 * members * rows * depth * heads * HD * 100,
            bytes_accessed=0 if early else 2 * depth * (members * rows + heads * 2 * HD),
            transcendentals=0,
        ),
        name="project_early" if early else "project_late",
    )(table, *arrays, *pieces, *extra)


def share_kernel(mine_ref, got_ref, own_ref, *out_refs):
    own_ref[...] = mine_ref[0] + got_ref[0]
    for k, out_ref in enumerate(out_refs):
        total = mine_ref[k + 1] + got_ref[k + 1]
        out_ref[:, : 2 * HD] = total.astype(jnp.bfloat16)
        keys = total[:, :HD]
        rest = keys - keys.astype(jnp.bfloat16).astype(jnp.float32)
        out_ref[:, 2 * HD :] = rest.astype(jnp.bfloat16)


def shares(mine, got):
    members, rows, columns = mine.shape
    out = jax.ShapeDtypeStruct((rows, columns + HD), jnp.bfloat16)
    vmem = pl.BlockSpec(memory_space=pltpu.VMEM)
    return pl.pallas_call(
        share_kernel,
        in_specs=[vmem] * 2,
        out_specs=[vmem] * members,
        out_shape=[jax.ShapeDtypeStruct((rows, columns), jnp.float32)] + [out] * (members - 1),
        compiler_params=pltpu.CompilerParams(vmem_limit_bytes=16 * MIB),
        name="shares",
    )(mine, got)


def sum_kernel(place_ref, *refs):
    out_ref = refs[-1]
    for k, group in enumerate((refs[:4], refs[4:8])):
        keys, values = group[0][:, :HD], group[0][:, HD:]
        for ref in group[1:]:
            rest = ref[:, 2 * HD :].astype(jnp.float32)
            keys = keys + (ref[:, :HD].astype(jnp.float32) + rest)
            values = values + ref[:, HD : 2 * HD].astype(jnp.float32)
        first = pl.multiple_of(jnp.bitwise_xor(place_ref[0], k) * 2 * HD, 2 * HD)
        out_ref[:, pl.ds(first, HD)] = keys.astype(jnp.bfloat16)
        out_ref[:, pl.ds(pl.multiple_of(first + HD, HD), HD)] = values.astype(jnp.bfloat16)


def summed(zz, straight, flipped):
    rows = straight[0].shape[0]
    vmem = pl.BlockSpec(memory_space=pltpu.VMEM)
    return pl.pallas_call(
        sum_kernel,
        in_specs=[pl.BlockSpec(memory_space=pltpu.SMEM)] + [vmem] * 8,
        out_specs=vmem,
        out_shape=jax.ShapeDtypeStruct((rows, 4 * HD), jnp.bfloat16),
        compiler_params=pltpu.CompilerParams(vmem_limit_bytes=16 * MIB),
        name="sum",
    )(zz.astype(jnp.int32)[None], *straight, *flipped)


def keyval_by_steps(sizes, hidden, codes, scales, segment_ids):
    rows = hidden.shape[0]
    hi, zz, y = lax.axis_index("hi"), lax.axis_index("zz"), lax.axis_index("y")
    shard = (hi * 2 + zz) * 2 + y
    same = (hi == lax.axis_index("tensor")).astype(jnp.int32)
    arrays, copies, piece = gather_by_steps(sizes, hidden, codes, scales, segment_ids)
    numbers = [c[2] for c in copies] + [y, same]
    table = jnp.stack([jnp.asarray(n, jnp.int32) for n in numbers])
    swap = flat_pairs(sizes, lambda g, s, c: (g, s, 1 - c))
    over_z = flat_pairs(sizes, lambda g, s, c: (g, s ^ 2, c))
    over_x = flat_pairs(sizes, lambda g, s, c: (1 - g, s, c))
    over_both = flat_pairs(sizes, lambda g, s, c: (1 - g, s ^ 2, c))

    def exchanged(mine, other):
        own, to_z, to_x, to_both = shares(mine, lax.ppermute(other, ALL, swap))
        return (
            own,
            lax.ppermute(to_both, ALL, over_both),
            lax.ppermute(to_z, ALL, over_z),
            lax.ppermute(to_x, ALL, over_x),
        )

    order = (2, 3, 6, 7, 0, 1)
    mine, other, own, ids = project_heads(
        True, arrays, copies, [piece[d] for d in order], table, rows
    )
    flipped = exchanged(mine, other)
    mine, other, last = project_heads(
        False, arrays, copies, [piece[4], piece[5]], table, rows, own
    )
    straight = exchanged(mine, other)
    keyval = summed(
        zz,
        (straight[0], flipped[1], flipped[2], straight[3]),
        (flipped[0], straight[1], straight[2], flipped[3]),
    )
    known = jnp.concatenate([ids, last], axis=0)[:, 0]
    place = jnp.asarray([(order + (4, 5)).index(d) for d in range(8)], jnp.int32)
    known = known[place[jnp.bitwise_xor(shard, jnp.arange(8, dtype=jnp.int32))]]
    return keyval, known


def gather_whole(sizes, hidden, codes, scales, segment_ids):
    groups = sizes[0]
    pair = lax.axis_size("zz")
    members = groups * pair
    rows, features = hidden.shape
    depth = features // members
    width = codes.shape[1]
    shards = sizes[1]
    shard = lax.axis_index(SHARD)
    share = pair * depth
    sliced = jnp.moveaxis(hidden.reshape(rows, members, depth), 1, 0)
    got = lax.all_to_all(sliced, BLOCK, 0, 0, tiled=True).reshape(members * rows, depth)
    copies = [(0, m * rows, 0, m) for m in range(members)]

    blocks = share // BLK
    group = lax.axis_index("groups")
    column = lax.dynamic_slice_in_dim(scales, (shard * width) // BLK, 1, 1)
    column = lax.dynamic_slice_in_dim(column, group * blocks, blocks, 0)
    held = lax.dynamic_slice_in_dim(codes, group * share, share, 0)
    weight = (held.astype(jnp.float32).reshape(blocks, BLK, width) * column[:, :, None]).astype(
        jnp.bfloat16
    )
    weight = weight.reshape(pair, depth, width)
    ids = segment_ids.astype(jnp.bfloat16).reshape(rows // width, width)
    ids = jnp.pad(ids, ((0, PAD - rows // width), (0, 0)))
    weight = jnp.concatenate([weight, jnp.broadcast_to(ids, (pair, PAD, width))], axis=1)
    high = lax.axis_size("hi")
    weight = jnp.broadcast_to(weight[None], (high,) + weight.shape)
    weight = weight.reshape(high * pair, depth + PAD, width)
    weight = lax.all_to_all(weight, ("hi", "zz"), 0, 0, tiled=True)
    weight = lax.all_gather(weight, "y", axis=1).reshape(shards, depth + PAD, width)
    known = weight[:, depth : depth + rows // width, :].reshape(shards, rows)
    weight = jnp.moveaxis(weight[:, :depth].reshape(2, shards // 2, depth, width), 1, 2)
    halves = weight.reshape(2, depth, shards * width // 2)
    return [got], copies, [halves[0], halves[1]], jnp.arange(2, dtype=jnp.int32), known


def project_kernel(copies, sources, columns, rows_ref, first_ref, member_ref, shard_ref, core_ref, *refs):
    hidden_refs, refs = refs[:sources], refs[sources:]
    weight_refs, (other_ref, mine_ref, left, halves, sems) = refs[:-5], refs[-5:]
    step = pl.program_id(0)
    rows = mine_ref.shape[1]
    depth = left.shape[1]
    core = core_ref[0]

    @pl.when(step == 0)
    def _():
        started = []
        for k, at in enumerate(copies):
            first = pl.multiple_of(first_ref[k], 128)
            row = pl.multiple_of(rows_ref[k], 16)
            to = pl.multiple_of(member_ref[k] * rows, rows)
            started.append(
                pltpu.make_async_copy(
                    hidden_refs[at].at[pl.ds(row, rows), pl.ds(first, depth)],
                    left.at[pl.ds(to, rows), :],
                    sems.at[k],
                )
            )
        for k, ref in enumerate(weight_refs):
            width = ref.shape[1]
            first = shard_ref[k] * width
            half = jnp.bitwise_xor(core, first // columns)
            at = pl.multiple_of(first % columns, 128)
            started.append(
                pltpu.make_async_copy(
                    ref.at[pl.ds(0, depth), :],
                    halves.at[half, :, pl.ds(at, width)],
                    sems.at[len(copies) + k],
                )
            )
        for copy in started:
            copy.start()
        for copy in started:
            copy.wait()

    size = mine_ref.shape[2]
    per_half = columns // size
    for half, out_ref in ((1, other_ref), (0, mine_ref)):
        for k in range(per_half):

            @pl.when(step == (1 - half) * per_half + k)
            def _():
                total = jnp.dot(
                    left[...],
                    halves[half, :, k * size : (k + 1) * size],
                    preferred_element_type=jnp.float32,
                )
                out_ref[...] = total.reshape(out_ref.shape)


def project(arrays, copies, pieces, shards, core, rows):
    members = len(copies)
    width = pieces[0].shape[1]
    columns = len(pieces) * width // 2
    depth = arrays[-1].shape[1]
    table = [jnp.stack([jnp.asarray(c[i], jnp.int32) for c in copies]) for i in (1, 2, 3)]
    size = 256
    per_half = columns // size
    out = jax.ShapeDtypeStruct((members, rows, columns), jnp.float32)
    return pl.pallas_call(
        functools.partial(project_kernel, [c[0] for c in copies], len(arrays), columns),
        grid_spec=pltpu.PrefetchScalarGridSpec(
            num_scalar_prefetch=5,
            grid=(2 * per_half,),
            in_specs=[pl.BlockSpec(memory_space=pl.ANY)] * (len(arrays) + len(pieces)),
            out_specs=[
                pl.BlockSpec((members, rows, size), lambda i, *_: (0, 0, jnp.minimum(i, per_half - 1))),
                pl.BlockSpec((members, rows, size), lambda i, *_: (0, 0, jnp.maximum(i - per_half, 0))),
            ],
            scratch_shapes=[
                pltpu.VMEM((members * rows, depth), jnp.bfloat16),
                pltpu.VMEM((2, depth, columns), jnp.bfloat16),
                pltpu.SemaphoreType.DMA((len(copies) + len(pieces),)),
            ],
        ),
        out_shape=[out, out],
        compiler_params=pltpu.CompilerParams(vmem_limit_bytes=24 * MIB),
        name="project",
    )(*table, shards, core, *arrays, *pieces)


def split_kernel(mine_ref, got_ref, out_ref):
    total = mine_ref[...] + got_ref[...]
    columns = total.shape[2]
    out_ref[:, :, :columns] = total.astype(jnp.bfloat16)
    for head in range(columns // (2 * HD)):
        keys = total[:, :, 2 * head * HD : (2 * head + 1) * HD]
        rest = keys - keys.astype(jnp.bfloat16).astype(jnp.float32)
        at = columns + head * HD
        out_ref[:, :, at : at + HD] = rest.astype(jnp.bfloat16)


def split(mine, got):
    members, rows, columns = mine.shape
    spec = pl.BlockSpec((1, rows, columns), lambda i: (i, 0, 0))
    wide = columns + columns // 2
    return pl.pallas_call(
        split_kernel,
        grid=(members,),
        in_specs=[spec, spec],
        out_specs=pl.BlockSpec((1, rows, wide), lambda i: (i, 0, 0)),
        out_shape=jax.ShapeDtypeStruct((members, rows, wide), jnp.bfloat16),
        compiler_params=pltpu.CompilerParams(vmem_limit_bytes=24 * MIB),
        name="split",
    )(mine, got)


def attend_kernel(pieces, heads, stack, query_ref, bias_ref, *refs):
    kv_refs, (out_ref, keys, values) = refs[:pieces], refs[pieces:]
    rows = query_ref.shape[0]
    scaling = math.log2(math.e) / math.sqrt(HD)
    for d, ref in enumerate(kv_refs):
        keys[d * rows : (d + 1) * rows, :] = ref[:, :HD]
        values[d * rows : (d + 1) * rows, :] = ref[:, HD:]
    bias = jnp.concatenate([bias_ref[...]] * stack, axis=0)
    for part in range(heads // stack):
        columns = [slice((part * stack + h) * HD, (part * stack + h + 1) * HD) for h in range(stack)]
        query = jnp.concatenate([query_ref[:, c] for c in columns], axis=0)
        scores = lax.dot_general(
            query, keys[...], (((1,), (1,)), ((), ())), preferred_element_type=jnp.float32
        )
        scores = scores + bias
        weights = jnp.exp2((scores - jnp.max(scores, axis=1, keepdims=True)) * scaling)
        totals = jnp.sum(weights, axis=1, keepdims=True)
        result = jnp.dot(
            weights.astype(jnp.bfloat16), values[...], preferred_element_type=jnp.float32
        )
        result = (result / totals).astype(jnp.bfloat16)
        for h, c in enumerate(columns):
            out_ref[:, c] = result[h * rows : (h + 1) * rows]


def attend(queries, bias, pieces):
    rows, width = queries.shape
    window = bias.shape[1]
    group = QPK * HD
    stack = 4 if window <= 1024 else 1
    return pl.pallas_call(
        functools.partial(attend_kernel, len(pieces), QPK, stack),
        grid=(width // group,),
        in_specs=[
            pl.BlockSpec((rows, group), lambda i: (0, i)),
            pl.BlockSpec((rows, window), lambda i: (0, 0)),
        ]
        + [pl.BlockSpec((rows, 2 * HD), lambda i: (0, i))] * len(pieces),
        out_specs=pl.BlockSpec((rows, group), lambda i: (0, i)),
        out_shape=jax.ShapeDtypeStruct((rows, width), jnp.bfloat16),
        scratch_shapes=[pltpu.VMEM((window, HD), jnp.bfloat16)] * 2,
        compiler_params=pltpu.CompilerParams(vmem_limit_bytes=24 * MIB),
        name="attend",
    )(queries, bias, *pieces)


def keyval_whole(sizes, hidden, codes, scales, segment_ids):
    rows = hidden.shape[0]
    core = lax.axis_index("tensor").astype(jnp.int32)
    arrays, copies, pieces, where, known = gather_whole(sizes, hidden, codes, scales, segment_ids)
    other, mine = project(arrays, copies, pieces, where, core[None], rows)
    swap = flat_pairs(sizes, lambda g, s, c: (g, s, 1 - c))
    partial = split(mine, lax.ppermute(other, ALL, swap))
    partial = lax.all_to_all(partial, BLOCK, 0, 0, tiled=True)
    total = jnp.sum(partial.astype(jnp.float32), axis=0)
    columns = mine.shape[2]
    rest = total[:, columns:].reshape(rows, -1, 1, HD)
    rest = jnp.concatenate([rest, jnp.zeros_like(rest)], axis=2).reshape(rows, columns)
    return (total[:, :columns] + rest).astype(jnp.bfloat16), known


def on_device(sizes, hidden, codes, scales, queries, segment_ids):
    groups, shards, cores = sizes
    rows = hidden.shape[0]
    shard = lax.axis_index(SHARD)
    by_steps = groups == 2 and shards == 8 and codes.shape[1] == BLK and rows == BLK
    make = keyval_by_steps if by_steps else keyval_whole
    keyval, known = make(sizes, hidden, codes, scales, segment_ids)

    back = min(shards // 2 + 1, shards - 1)
    from_shard = shard - jnp.arange(back + 1, dtype=jnp.int32)
    seen = known[jnp.maximum(from_shard, 0)].reshape(-1)
    offset = jnp.arange(rows, dtype=jnp.int32)
    keypos = (from_shard[:, None] * rows + offset[None, :]).reshape(-1)
    rowpos = shard * rows + offset
    allowed = (
        (segment_ids.astype(jnp.bfloat16)[:, None] == seen[None, :])
        & (keypos[None, :] <= rowpos[:, None])
        & (keypos[None, :] >= 0)
    )
    bias = jnp.where(allowed, 0.0, -jnp.inf).astype(jnp.float32)

    pieces = [keyval]
    for d in range(1, back + 1):
        up = flat_pairs(sizes, lambda g, s, c: (g, s + d, c) if s + d < shards else None)
        pieces.append(lax.ppermute(keyval, ALL, up))
    return attend(queries, bias, pieces)


def solution(mesh):
    sizes = tuple(mesh.shape[name] for name in ("groups", "shard", "tensor"))
    groups, shards, cores = sizes
    y = math.gcd(shards, 2)
    zz = math.gcd(shards // y, 2)
    fine = Mesh(mesh.devices.reshape(groups, shards // (y * zz), zz, y, cores), ALL)
    tokens = ("groups",) + SHARD
    in_specs = (
        P(tokens, "tensor"),
        P("tensor", SHARD),
        P("tensor", None),
        P(tokens, "tensor"),
        P(tokens),
    )
    return jax.shard_map(
        functools.partial(on_device, sizes),
        mesh=fine,
        in_specs=in_specs,
        out_specs=P(tokens, "tensor"),
        check_vma=False,
    )
```

```python
import functools
import math

import jax
import jax.numpy as jnp
from jax import lax
from jax.experimental import pallas as pl
from jax.experimental.pallas import tpu as pltpu
from jax.sharding import Mesh
from jax.sharding import PartitionSpec as P

KVH = 4
HD = 128
QPK = 16
BLK = 128
KVW = 1024
PAD = 16
SHARD = ("hi", "zz", "y")
ALL = ("groups",) + SHARD + ("tensor",)
BLOCK = ("groups", "zz")
MIB = 2**20


def gate_kernel(value_ref, *refs):
    pass


def gate(value, *others):
    hbm = pl.BlockSpec(memory_space=pl.ANY)
    return pl.pallas_call(
        gate_kernel,
        in_specs=[hbm] * (1 + len(others)),
        out_specs=hbm,
        out_shape=jax.ShapeDtypeStruct(value.shape, value.dtype),
        input_output_aliases={0: 0},
        compiler_params=pltpu.CompilerParams(vmem_limit_bytes=MIB),
        name="gate",
    )(value, *others)


def flat_pairs(sizes, move):
    groups, shards, cores = sizes
    pairs = []
    for g in range(groups):
        for s in range(shards):
            for c in range(cores):
                to = move(g, s, c)
                if to is not None:
                    pairs.append(((g * shards + s) * cores + c, (to[0] * shards + to[1]) * cores + to[2]))
    return pairs


def scale_kernel(first_ref, codes_ref, scales_ref, ids_ref, near_ref, far_ref, copy_ref, held, sems):
    depth = near_ref.shape[0] - PAD
    blocks = depth // BLK
    own, column, block = first_ref[0], first_ref[1], first_ref[2]
    copies = []
    for k, which in enumerate((1 - own, own)):
        row = pl.multiple_of((block + which * blocks) * BLK, BLK)
        copies.append(
            pltpu.make_async_copy(codes_ref.at[pl.ds(row, depth), :], held.at[k], sems.at[k])
        )
        copies[k].start()
    ids = ids_ref[...].astype(jnp.float32)
    ids = jnp.broadcast_to(ids, (PAD, ids.shape[1])).astype(jnp.bfloat16)
    for k, (out_ref, which) in enumerate(((far_ref, 1 - own), (near_ref, own))):
        copies[k].wait()
        for b in range(blocks):
            scale = scales_ref[column, block + which * blocks + b]
            part = held[k, b * BLK : (b + 1) * BLK, :].astype(jnp.float32) * scale
            out_ref[b * BLK : (b + 1) * BLK, :] = part.astype(jnp.bfloat16)
        out_ref[depth:, :] = ids
    copy_ref[...] = near_ref[...]


def scaled_weight(codes, scales, segment_ids, depth, group, zz, column):
    width = codes.shape[1]
    first = jnp.stack([zz, column, group * (2 * depth // BLK)]).astype(jnp.int32)
    out = jax.ShapeDtypeStruct((depth + PAD, width), jnp.bfloat16)
    return pl.pallas_call(
        scale_kernel,
        in_specs=[
            pl.BlockSpec(memory_space=pltpu.SMEM),
            pl.BlockSpec(memory_space=pltpu.HBM),
            pl.BlockSpec(memory_space=pltpu.SMEM),
            pl.BlockSpec(memory_space=pltpu.VMEM),
        ],
        out_specs=[pl.BlockSpec(memory_space=pltpu.VMEM)] * 3,
        out_shape=[out, out, out],
        scratch_shapes=[
            pltpu.VMEM((2, depth, width), jnp.bfloat16),
            pltpu.SemaphoreType.DMA((2,)),
        ],
        compiler_params=pltpu.CompilerParams(vmem_limit_bytes=56 * MIB),
        name="scale",
    )(first, codes, scales.T, segment_ids.reshape(1, -1))


def gather_by_steps(sizes, hidden, codes, scales, segment_ids):
    rows, features = hidden.shape
    depth = features // 4
    group, zz, y = lax.axis_index("groups"), lax.axis_index("zz"), lax.axis_index("y")
    shard = (lax.axis_index("hi") * 2 + zz) * 2 + y
    member = group * 2 + zz

    def send(value, move):
        return lax.ppermute(value, ALL, flat_pairs(sizes, move))

    def along_shard(distance):
        return lambda g, s, c: (g, s ^ distance, c)

    near, far, later = scaled_weight(
        codes, scales, segment_ids, depth, group, zz, shard * codes.shape[1] // BLK
    )
    def quarter(dg, dz):
        first = (jnp.bitwise_xor(group, dg) * 2 + jnp.bitwise_xor(zz, dz)) * depth
        return lax.dynamic_slice_in_dim(hidden, first, depth, 1)

    across = send(quarter(1, 1), lambda g, s, c: (1 - g, s, c))
    stays = send(quarter(1, 0), lambda g, s, c: (1 - g, s, c))
    piece = {0: near}
    piece[6] = send(far, along_shard(6))
    piece[2] = send(far, along_shard(2))
    piece[1] = send(near, along_shard(1))
    piece[4] = send(gate(later, piece[2]), along_shard(4))
    pair = jnp.concatenate(
        [
            lax.dynamic_slice_in_dim(hidden, (group * 2 + 1 - zz) * depth, depth, 1),
            across,
        ],
        axis=0,
    )
    pair = send(pair, along_shard(2))
    piece[3] = send(piece[2], along_shard(1))
    piece[6] = gate(piece[6], piece[3])
    piece[7] = send(piece[6], along_shard(1))
    piece[5] = send(piece[4], along_shard(1))
    arrays = [hidden, stays, pair]
    copies = [(0, 0, member * depth), (2, 0, 0), (1, 0, 0), (2, rows, 0)]
    return arrays, copies, piece


def head_kernel(copies, heads, early, table_ref, *refs):
    hidden_refs, refs = refs[:3], refs[3:]
    weight_refs, refs = refs[: 2 * heads], refs[2 * heads :]
    if early:
        mine_ref, other_ref, own_ref, ids_ref, left, right, sems = refs
    else:
        own_ref, mine_ref, other_ref, ids_ref, left, right, sems = refs
    rows, depth = mine_ref.shape[1], left.shape[1]
    count = len(copies)
    started = []
    for k, (at, row) in enumerate(copies):
        first = pl.multiple_of(table_ref[k], HD)
        started.append(
            pltpu.make_async_copy(
                hidden_refs[at].at[row : row + rows, pl.ds(first, depth)],
                left.at[k * rows : (k + 1) * rows, :],
                sems.at[k],
            )
        )
    for k, ref in enumerate(weight_refs):
        first = pl.multiple_of(jnp.bitwise_xor(table_ref[count], k % 2) * HD, HD)
        started.append(
            pltpu.make_async_copy(
                ref.at[pl.ds(0, depth), :], right.at[k // 2, :, pl.ds(first, HD)], sems.at[count + k]
            )
        )
    for k, ref in enumerate(weight_refs):
        started.append(
            pltpu.make_async_copy(
                ref.at[pl.ds(depth, PAD), :], ids_ref.at[k], sems.at[count + 2 * heads + k]
            )
        )
    for copy in started:
        copy.start()
    for copy in started[:count]:
        copy.wait()

    def head(h):
        for copy in started[count + 2 * h : count + 2 * h + 2]:
            copy.wait()
        total = jnp.dot(left[...], right[h], preferred_element_type=jnp.float32)
        return total.reshape(mine_ref.shape)

    def put(here, there, first, second):
        @pl.when(table_ref[count + 1] == 1)
        def _():
            here[...] = first
            if second is not None:
                there[...] = second

        @pl.when(table_ref[count + 1] == 0)
        def _():
            there[...] = first
            if second is not None:
                here[...] = second

    if early:
        put(mine_ref, other_ref, head(0), None)
        put(other_ref, mine_ref, head(1), None)
        own_ref[...] = head(2)
    else:
        put(mine_ref, other_ref, own_ref[...], head(0))
    for copy in started[count + 2 * heads :]:
        copy.wait()


def project_heads(early, arrays, copies, pieces, table, rows, own=None):
    heads = len(pieces) // 2
    depth = arrays[-1].shape[1]
    members = len(copies)
    out = jax.ShapeDtypeStruct((members, rows, 2 * HD), jnp.float32)
    ids = jax.ShapeDtypeStruct((len(pieces), PAD, HD), jnp.bfloat16)
    vmem = pl.BlockSpec(memory_space=pltpu.VMEM)
    extra = [] if early else [own]
    results = [out] * (3 if early else 2) + [ids]
    return pl.pallas_call(
        functools.partial(head_kernel, [c[:2] for c in copies], heads, early),
        in_specs=[pl.BlockSpec(memory_space=pltpu.SMEM)]
        + [pl.BlockSpec(memory_space=pl.ANY)] * (len(arrays) + len(pieces))
        + [vmem] * len(extra),
        out_specs=[vmem] * len(results),
        out_shape=results,
        scratch_shapes=[
            pltpu.VMEM((members * rows, depth), jnp.bfloat16),
            pltpu.VMEM((heads, depth, 2 * HD), jnp.bfloat16),
            pltpu.SemaphoreType.DMA((members + 2 * len(pieces),)),
        ],
        compiler_params=pltpu.CompilerParams(vmem_limit_bytes=24 * MIB),
        cost_estimate=pl.CostEstimate(
            flops=0 if early else 4 * members * rows * depth * heads * HD * 100,
            bytes_accessed=0 if early else 2 * depth * (members * rows + heads * 2 * HD),
            transcendentals=0,
        ),
        name="project_early" if early else "project_late",
    )(table, *arrays, *pieces, *extra)


def share_kernel(mine_ref, got_ref, own_ref, *out_refs):
    own_ref[...] = mine_ref[0] + got_ref[0]
    for k, out_ref in enumerate(out_refs):
        total = mine_ref[k + 1] + got_ref[k + 1]
        out_ref[:, : 2 * HD] = total.astype(jnp.bfloat16)
        keys = total[:, :HD]
        rest = keys - keys.astype(jnp.bfloat16).astype(jnp.float32)
        out_ref[:, 2 * HD :] = rest.astype(jnp.bfloat16)


def shares(mine, got):
    members, rows, columns = mine.shape
    out = jax.ShapeDtypeStruct((rows, columns + HD), jnp.bfloat16)
    vmem = pl.BlockSpec(memory_space=pltpu.VMEM)
    return pl.pallas_call(
        share_kernel,
        in_specs=[vmem] * 2,
        out_specs=[vmem] * members,
        out_shape=[jax.ShapeDtypeStruct((rows, columns), jnp.float32)] + [out] * (members - 1),
        compiler_params=pltpu.CompilerParams(vmem_limit_bytes=16 * MIB),
        name="shares",
    )(mine, got)


def sum_kernel(place_ref, *refs):
    out_ref = refs[-1]
    for k, group in enumerate((refs[:4], refs[4:8])):
        keys, values = group[0][:, :HD], group[0][:, HD:]
        for ref in group[1:]:
            rest = ref[:, 2 * HD :].astype(jnp.float32)
            keys = keys + (ref[:, :HD].astype(jnp.float32) + rest)
            values = values + ref[:, HD : 2 * HD].astype(jnp.float32)
        first = pl.multiple_of(jnp.bitwise_xor(place_ref[0], k) * 2 * HD, 2 * HD)
        out_ref[:, pl.ds(first, HD)] = keys.astype(jnp.bfloat16)
        out_ref[:, pl.ds(pl.multiple_of(first + HD, HD), HD)] = values.astype(jnp.bfloat16)


def summed(zz, straight, flipped):
    rows = straight[0].shape[0]
    vmem = pl.BlockSpec(memory_space=pltpu.VMEM)
    return pl.pallas_call(
        sum_kernel,
        in_specs=[pl.BlockSpec(memory_space=pltpu.SMEM)] + [vmem] * 8,
        out_specs=vmem,
        out_shape=jax.ShapeDtypeStruct((rows, 4 * HD), jnp.bfloat16),
        compiler_params=pltpu.CompilerParams(vmem_limit_bytes=16 * MIB),
        name="sum",
    )(zz.astype(jnp.int32)[None], *straight, *flipped)


def keyval_by_steps(sizes, hidden, codes, scales, segment_ids):
    rows = hidden.shape[0]
    hi, zz, y = lax.axis_index("hi"), lax.axis_index("zz"), lax.axis_index("y")
    shard = (hi * 2 + zz) * 2 + y
    same = (hi == lax.axis_index("tensor")).astype(jnp.int32)
    arrays, copies, piece = gather_by_steps(sizes, hidden, codes, scales, segment_ids)
    numbers = [c[2] for c in copies] + [y, same]
    table = jnp.stack([jnp.asarray(n, jnp.int32) for n in numbers])
    swap = flat_pairs(sizes, lambda g, s, c: (g, s, 1 - c))
    over_z = flat_pairs(sizes, lambda g, s, c: (g, s ^ 2, c))
    over_x = flat_pairs(sizes, lambda g, s, c: (1 - g, s, c))
    over_both = flat_pairs(sizes, lambda g, s, c: (1 - g, s ^ 2, c))

    def exchanged(mine, other):
        own, to_z, to_x, to_both = shares(mine, lax.ppermute(other, ALL, swap))
        return (
            own,
            lax.ppermute(to_both, ALL, over_both),
            lax.ppermute(to_z, ALL, over_z),
            lax.ppermute(to_x, ALL, over_x),
        )

    order = (2, 3, 6, 7, 0, 1)
    mine, other, own, ids = project_heads(
        True, arrays, copies, [piece[d] for d in order], table, rows
    )
    flipped = exchanged(mine, other)
    mine, other, last = project_heads(
        False, arrays, copies, [piece[4], piece[5]], table, rows, own
    )
    straight = exchanged(mine, other)
    keyval = summed(
        zz,
        (straight[0], flipped[1], flipped[2], straight[3]),
        (flipped[0], straight[1], straight[2], flipped[3]),
    )
    known = jnp.concatenate([ids, last], axis=0)[:, 0]
    place = jnp.asarray([(order + (4, 5)).index(d) for d in range(8)], jnp.int32)
    known = known[place[jnp.bitwise_xor(shard, jnp.arange(8, dtype=jnp.int32))]]
    return keyval, known


def gather_whole(sizes, hidden, codes, scales, segment_ids):
    groups = sizes[0]
    pair = lax.axis_size("zz")
    members = groups * pair
    rows, features = hidden.shape
    depth = features // members
    width = codes.shape[1]
    shards = sizes[1]
    shard = lax.axis_index(SHARD)
    share = pair * depth
    sliced = jnp.moveaxis(hidden.reshape(rows, members, depth), 1, 0)
    got = lax.all_to_all(sliced, BLOCK, 0, 0, tiled=True).reshape(members * rows, depth)
    copies = [(0, m * rows, 0, m) for m in range(members)]

    blocks = share // BLK
    group = lax.axis_index("groups")
    column = lax.dynamic_slice_in_dim(scales, (shard * width) // BLK, 1, 1)
    column = lax.dynamic_slice_in_dim(column, group * blocks, blocks, 0)
    held = lax.dynamic_slice_in_dim(codes, group * share, share, 0)
    weight = (held.astype(jnp.float32).reshape(blocks, BLK, width) * column[:, :, None]).astype(
        jnp.bfloat16
    )
    weight = weight.reshape(pair, depth, width)
    ids = segment_ids.astype(jnp.bfloat16).reshape(rows // width, width)
    ids = jnp.pad(ids, ((0, PAD - rows // width), (0, 0)))
    weight = jnp.concatenate([weight, jnp.broadcast_to(ids, (pair, PAD, width))], axis=1)
    high = lax.axis_size("hi")
    weight = jnp.broadcast_to(weight[None], (high,) + weight.shape)
    weight = weight.reshape(high * pair, depth + PAD, width)
    weight = lax.all_to_all(weight, ("hi", "zz"), 0, 0, tiled=True)
    weight = lax.all_gather(weight, "y", axis=1).reshape(shards, depth + PAD, width)
    known = weight[:, depth : depth + rows // width, :].reshape(shards, rows)
    weight = jnp.moveaxis(weight[:, :depth].reshape(2, shards // 2, depth, width), 1, 2)
    halves = weight.reshape(2, depth, shards * width // 2)
    return [got], copies, [halves[0], halves[1]], jnp.arange(2, dtype=jnp.int32), known


def project_kernel(copies, sources, columns, rows_ref, first_ref, member_ref, shard_ref, core_ref, *refs):
    hidden_refs, refs = refs[:sources], refs[sources:]
    weight_refs, (other_ref, mine_ref, left, halves, sems) = refs[:-5], refs[-5:]
    step = pl.program_id(0)
    rows = mine_ref.shape[1]
    depth = left.shape[1]
    core = core_ref[0]

    @pl.when(step == 0)
    def _():
        started = []
        for k, at in enumerate(copies):
            first = pl.multiple_of(first_ref[k], 128)
            row = pl.multiple_of(rows_ref[k], 16)
            to = pl.multiple_of(member_ref[k] * rows, rows)
            started.append(
                pltpu.make_async_copy(
                    hidden_refs[at].at[pl.ds(row, rows), pl.ds(first, depth)],
                    left.at[pl.ds(to, rows), :],
                    sems.at[k],
                )
            )
        for k, ref in enumerate(weight_refs):
            width = ref.shape[1]
            first = shard_ref[k] * width
            half = jnp.bitwise_xor(core, first // columns)
            at = pl.multiple_of(first % columns, 128)
            started.append(
                pltpu.make_async_copy(
                    ref.at[pl.ds(0, depth), :],
                    halves.at[half, :, pl.ds(at, width)],
                    sems.at[len(copies) + k],
                )
            )
        for copy in started:
            copy.start()
        for copy in started:
            copy.wait()

    size = mine_ref.shape[2]
    per_half = columns // size
    for half, out_ref in ((1, other_ref), (0, mine_ref)):
        for k in range(per_half):

            @pl.when(step == (1 - half) * per_half + k)
            def _():
                total = jnp.dot(
                    left[...],
                    halves[half, :, k * size : (k + 1) * size],
                    preferred_element_type=jnp.float32,
                )
                out_ref[...] = total.reshape(out_ref.shape)


def project(arrays, copies, pieces, shards, core, rows):
    members = len(copies)
    width = pieces[0].shape[1]
    columns = len(pieces) * width // 2
    depth = arrays[-1].shape[1]
    table = [jnp.stack([jnp.asarray(c[i], jnp.int32) for c in copies]) for i in (1, 2, 3)]
    size = 256
    per_half = columns // size
    out = jax.ShapeDtypeStruct((members, rows, columns), jnp.float32)
    return pl.pallas_call(
        functools.partial(project_kernel, [c[0] for c in copies], len(arrays), columns),
        grid_spec=pltpu.PrefetchScalarGridSpec(
            num_scalar_prefetch=5,
            grid=(2 * per_half,),
            in_specs=[pl.BlockSpec(memory_space=pl.ANY)] * (len(arrays) + len(pieces)),
            out_specs=[
                pl.BlockSpec((members, rows, size), lambda i, *_: (0, 0, jnp.minimum(i, per_half - 1))),
                pl.BlockSpec((members, rows, size), lambda i, *_: (0, 0, jnp.maximum(i - per_half, 0))),
            ],
            scratch_shapes=[
                pltpu.VMEM((members * rows, depth), jnp.bfloat16),
                pltpu.VMEM((2, depth, columns), jnp.bfloat16),
                pltpu.SemaphoreType.DMA((len(copies) + len(pieces),)),
            ],
        ),
        out_shape=[out, out],
        compiler_params=pltpu.CompilerParams(vmem_limit_bytes=24 * MIB),
        name="project",
    )(*table, shards, core, *arrays, *pieces)


def split_kernel(mine_ref, got_ref, out_ref):
    total = mine_ref[...] + got_ref[...]
    columns = total.shape[2]
    out_ref[:, :, :columns] = total.astype(jnp.bfloat16)
    for head in range(columns // (2 * HD)):
        keys = total[:, :, 2 * head * HD : (2 * head + 1) * HD]
        rest = keys - keys.astype(jnp.bfloat16).astype(jnp.float32)
        at = columns + head * HD
        out_ref[:, :, at : at + HD] = rest.astype(jnp.bfloat16)


def split(mine, got):
    members, rows, columns = mine.shape
    spec = pl.BlockSpec((1, rows, columns), lambda i: (i, 0, 0))
    wide = columns + columns // 2
    return pl.pallas_call(
        split_kernel,
        grid=(members,),
        in_specs=[spec, spec],
        out_specs=pl.BlockSpec((1, rows, wide), lambda i: (i, 0, 0)),
        out_shape=jax.ShapeDtypeStruct((members, rows, wide), jnp.bfloat16),
        compiler_params=pltpu.CompilerParams(vmem_limit_bytes=24 * MIB),
        name="split",
    )(mine, got)


def attend_kernel(pieces, heads, stack, query_ref, bias_ref, *refs):
    kv_refs, (out_ref, keys, values) = refs[:pieces], refs[pieces:]
    rows = query_ref.shape[0]
    scaling = math.log2(math.e) / math.sqrt(HD)
    for d, ref in enumerate(kv_refs):
        keys[d * rows : (d + 1) * rows, :] = ref[:, :HD]
        values[d * rows : (d + 1) * rows, :] = ref[:, HD:]
    bias = jnp.concatenate([bias_ref[...]] * stack, axis=0)
    for part in range(heads // stack):
        columns = [slice((part * stack + h) * HD, (part * stack + h + 1) * HD) for h in range(stack)]
        query = jnp.concatenate([query_ref[:, c] for c in columns], axis=0)
        scores = lax.dot_general(
            query, keys[...], (((1,), (1,)), ((), ())), preferred_element_type=jnp.float32
        )
        scores = scores + bias
        weights = jnp.exp2((scores - jnp.max(scores, axis=1, keepdims=True)) * scaling)
        totals = jnp.sum(weights, axis=1, keepdims=True)
        result = jnp.dot(
            weights.astype(jnp.bfloat16), values[...], preferred_element_type=jnp.float32
        )
        result = (result / totals).astype(jnp.bfloat16)
        for h, c in enumerate(columns):
            out_ref[:, c] = result[h * rows : (h + 1) * rows]


def attend(queries, bias, pieces):
    rows, width = queries.shape
    window = bias.shape[1]
    group = QPK * HD
    stack = 4 if window <= 1024 else 1
    return pl.pallas_call(
        functools.partial(attend_kernel, len(pieces), QPK, stack),
        grid=(width // group,),
        in_specs=[
            pl.BlockSpec((rows, group), lambda i: (0, i)),
            pl.BlockSpec((rows, window), lambda i: (0, 0)),
        ]
        + [pl.BlockSpec((rows, 2 * HD), lambda i: (0, i))] * len(pieces),
        out_specs=pl.BlockSpec((rows, group), lambda i: (0, i)),
        out_shape=jax.ShapeDtypeStruct((rows, width), jnp.bfloat16),
        scratch_shapes=[pltpu.VMEM((window, HD), jnp.bfloat16)] * 2,
        compiler_params=pltpu.CompilerParams(vmem_limit_bytes=24 * MIB),
        name="attend",
    )(queries, bias, *pieces)


def keyval_whole(sizes, hidden, codes, scales, segment_ids):
    rows = hidden.shape[0]
    core = lax.axis_index("tensor").astype(jnp.int32)
    arrays, copies, pieces, where, known = gather_whole(sizes, hidden, codes, scales, segment_ids)
    other, mine = project(arrays, copies, pieces, where, core[None], rows)
    swap = flat_pairs(sizes, lambda g, s, c: (g, s, 1 - c))
    partial = split(mine, lax.ppermute(other, ALL, swap))
    partial = lax.all_to_all(partial, BLOCK, 0, 0, tiled=True)
    total = jnp.sum(partial.astype(jnp.float32), axis=0)
    columns = mine.shape[2]
    rest = total[:, columns:].reshape(rows, -1, 1, HD)
    rest = jnp.concatenate([rest, jnp.zeros_like(rest)], axis=2).reshape(rows, columns)
    return (total[:, :columns] + rest).astype(jnp.bfloat16), known


def on_device(sizes, hidden, codes, scales, queries, segment_ids):
    groups, shards, cores = sizes
    rows = hidden.shape[0]
    shard = lax.axis_index(SHARD)
    by_steps = groups == 2 and shards == 8 and codes.shape[1] == BLK and rows == BLK
    make = keyval_by_steps if by_steps else keyval_whole
    keyval, known = make(sizes, hidden, codes, scales, segment_ids)

    back = min(shards // 2 + 1, shards - 1)
    from_shard = shard - jnp.arange(back + 1, dtype=jnp.int32)
    seen = known[jnp.maximum(from_shard, 0)].reshape(-1)
    offset = jnp.arange(rows, dtype=jnp.int32)
    keypos = (from_shard[:, None] * rows + offset[None, :]).reshape(-1)
    rowpos = shard * rows + offset
    allowed = (
        (segment_ids.astype(jnp.bfloat16)[:, None] == seen[None, :])
        & (keypos[None, :] <= rowpos[:, None])
        & (keypos[None, :] >= 0)
    )
    bias = jnp.where(allowed, 0.0, -jnp.inf).astype(jnp.float32)

    pieces = [keyval]
    for d in range(1, back + 1):
        up = flat_pairs(sizes, lambda g, s, c: (g, s + d, c) if s + d < shards else None)
        pieces.append(lax.ppermute(keyval, ALL, up))
    return attend(queries, bias, pieces)


def solution(mesh):
    sizes = tuple(mesh.shape[name] for name in ("groups", "shard", "tensor"))
    groups, shards, cores = sizes
    y = math.gcd(shards, 2)
    zz = math.gcd(shards // y, 2)
    fine = Mesh(mesh.devices.reshape(groups, shards // (y * zz), zz, y, cores), ALL)
    tokens = ("groups",) + SHARD
    in_specs = (
        P(tokens, "tensor"),
        P("tensor", SHARD),
        P("tensor", None),
        P(tokens, "tensor"),
        P(tokens),
    )
    return jax.shard_map(
        functools.partial(on_device, sizes),
        mesh=fine,
        in_specs=in_specs,
        out_specs=P(tokens, "tensor"),
        check_vma=False,
    )
```

```python
import functools
import math

import jax
import jax.numpy as jnp
from jax import lax
from jax.experimental import pallas as pl
from jax.experimental.pallas import tpu as pltpu
from jax.sharding import Mesh
from jax.sharding import PartitionSpec as P

KVH = 4
HD = 128
QPK = 16
BLK = 128
KVW = 1024
PAD = 16
SHARD = ("hi", "zz", "y")
ALL = ("groups",) + SHARD + ("tensor",)
BLOCK = ("groups", "zz")
MIB = 2**20


def gate_kernel(value_ref, *refs):
    pass


def gate(value, *others):
    hbm = pl.BlockSpec(memory_space=pl.ANY)
    return pl.pallas_call(
        gate_kernel,
        in_specs=[hbm] * (1 + len(others)),
        out_specs=hbm,
        out_shape=jax.ShapeDtypeStruct(value.shape, value.dtype),
        input_output_aliases={0: 0},
        compiler_params=pltpu.CompilerParams(vmem_limit_bytes=MIB),
        name="gate",
    )(value, *others)


def flat_pairs(sizes, move):
    groups, shards, cores = sizes
    pairs = []
    for g in range(groups):
        for s in range(shards):
            for c in range(cores):
                to = move(g, s, c)
                if to is not None:
                    pairs.append(((g * shards + s) * cores + c, (to[0] * shards + to[1]) * cores + to[2]))
    return pairs


def scale_kernel(codes_ref, scales_ref, ids_ref, near_ref, far_ref, copy_ref, held, factors, sems):
    depth = near_ref.shape[0] - PAD
    width = near_ref.shape[1]
    blocks = depth // BLK
    own = lax.axis_index("zz")
    shard = (lax.axis_index("hi") * lax.axis_size("zz") + own) * lax.axis_size("y") + lax.axis_index("y")
    column = shard * width // BLK
    block = lax.axis_index("groups") * 2 * blocks
    copies = [pltpu.make_async_copy(scales_ref, factors, sems.at[2])]
    for k, which in enumerate((1 - own, own)):
        row = pl.multiple_of((block + which * blocks) * BLK, BLK)
        copies.append(
            pltpu.make_async_copy(codes_ref.at[pl.ds(row, depth), :], held.at[k], sems.at[k])
        )
    for copy in copies:
        copy.start()
    ids = ids_ref[...].astype(jnp.float32)
    ids = jnp.broadcast_to(ids, (PAD, ids.shape[1])).astype(jnp.bfloat16)
    copies[0].wait()
    for k, (out_ref, which) in enumerate(((far_ref, 1 - own), (near_ref, own))):
        copies[k + 1].wait()
        for b in range(blocks):
            scale = factors[column, block + which * blocks + b]
            part = held[k, b * BLK : (b + 1) * BLK, :].astype(jnp.float32) * scale
            out_ref[b * BLK : (b + 1) * BLK, :] = part.astype(jnp.bfloat16)
        out_ref[depth:, :] = ids
    copy_ref[...] = near_ref[...]


def scaled_weight(codes, scales, segment_ids, depth):
    width = codes.shape[1]
    out = jax.ShapeDtypeStruct((depth + PAD, width), jnp.bfloat16)
    return pl.pallas_call(
        scale_kernel,
        in_specs=[
            pl.BlockSpec(memory_space=pltpu.HBM),
            pl.BlockSpec(memory_space=pltpu.HBM),
            pl.BlockSpec(memory_space=pltpu.VMEM),
        ],
        out_specs=[pl.BlockSpec(memory_space=pltpu.VMEM)] * 3,
        out_shape=[out, out, out],
        scratch_shapes=[
            pltpu.VMEM((2, depth, width), jnp.bfloat16),
            pltpu.SMEM(scales.shape[::-1], jnp.float32),
            pltpu.SemaphoreType.DMA((3,)),
        ],
        compiler_params=pltpu.CompilerParams(vmem_limit_bytes=56 * MIB),
        name="scale",
    )(codes, scales.T, segment_ids.reshape(1, -1))


def gather_by_steps(sizes, hidden, codes, scales, segment_ids):
    rows, features = hidden.shape
    depth = features // 4
    group, zz, y = lax.axis_index("groups"), lax.axis_index("zz"), lax.axis_index("y")
    shard = (lax.axis_index("hi") * 2 + zz) * 2 + y
    member = group * 2 + zz

    def send(value, move):
        return lax.ppermute(value, ALL, flat_pairs(sizes, move))

    def along_shard(distance):
        return lambda g, s, c: (g, s ^ distance, c)

    near, far, later = scaled_weight(codes, scales, segment_ids, depth)
    piece = {0: near}
    def quarter(dg, dz):
        first = (jnp.bitwise_xor(group, dg) * 2 + jnp.bitwise_xor(zz, dz)) * depth
        return lax.dynamic_slice_in_dim(hidden, first, depth, 1)

    across = send(quarter(1, 1), lambda g, s, c: (1 - g, s, c))
    stays = send(quarter(1, 0), lambda g, s, c: (1 - g, s, c))
    piece[6] = send(far, along_shard(6))
    piece[1] = send(near, along_shard(1))
    piece[2] = send(far, along_shard(2))
    piece[4] = send(gate(later, piece[2]), along_shard(4))
    pair = jnp.concatenate(
        [
            lax.dynamic_slice_in_dim(hidden, (group * 2 + 1 - zz) * depth, depth, 1),
            across,
        ],
        axis=0,
    )
    pair = send(gate(pair, piece[1]), along_shard(2))
    piece[3] = send(piece[2], along_shard(1))
    piece[6] = gate(piece[6], piece[3], stays)
    piece[7] = send(piece[6], along_shard(1))
    piece[4] = gate(piece[4], stays)
    piece[5] = send(piece[4], along_shard(1))
    arrays = [hidden, stays, pair]
    copies = [(0, 0, member * depth), (2, 0, 0), (1, 0, 0), (2, rows, 0)]
    return arrays, copies, piece


def head_kernel(copies, heads, early, table_ref, *refs):
    hidden_refs, refs = refs[:3], refs[3:]
    weight_refs, refs = refs[: 2 * heads], refs[2 * heads :]
    if early:
        mine_ref, other_ref, own_ref, ids_ref, left, right, sems = refs
    else:
        own_ref, left, mine_ref, other_ref, ids_ref, right, sems = refs
    rows, depth = mine_ref.shape[1], left.shape[1]
    count = len(copies)
    started = []
    for k, (at, row) in enumerate(copies if early else []):
        first = pl.multiple_of(table_ref[k], HD)
        started.append(
            pltpu.make_async_copy(
                hidden_refs[at].at[row : row + rows, pl.ds(first, depth)],
                left.at[k * rows : (k + 1) * rows, :],
                sems.at[k],
            )
        )
    for k, ref in enumerate(weight_refs):
        first = pl.multiple_of(jnp.bitwise_xor(table_ref[count], k % 2) * HD, HD)
        started.append(
            pltpu.make_async_copy(
                ref.at[pl.ds(0, depth), :], right.at[k // 2, :, pl.ds(first, HD)], sems.at[count + k]
            )
        )
    for k, ref in enumerate(weight_refs):
        started.append(
            pltpu.make_async_copy(
                ref.at[pl.ds(depth, PAD), :], ids_ref.at[k], sems.at[count + 2 * heads + k]
            )
        )
    for copy in started:
        copy.start()
    moved = count if early else 0
    for copy in started[:moved]:
        copy.wait()

    def head(h):
        for copy in started[moved + 2 * h : moved + 2 * h + 2]:
            copy.wait()
        total = jnp.dot(left[...], right[h], preferred_element_type=jnp.float32)
        return total.reshape(mine_ref.shape)

    def put(here, there, first, second):
        @pl.when(table_ref[count + 1] == 1)
        def _():
            here[...] = first
            if second is not None:
                there[...] = second

        @pl.when(table_ref[count + 1] == 0)
        def _():
            there[...] = first
            if second is not None:
                here[...] = second

    if early:
        put(mine_ref, other_ref, head(0), None)
        put(other_ref, mine_ref, head(1), None)
        own_ref[...] = head(2)
    else:
        put(mine_ref, other_ref, own_ref[...], head(0))
    for copy in started[moved + 2 * heads :]:
        copy.wait()


def project_heads(early, arrays, copies, pieces, table, rows, held=()):
    heads = len(pieces) // 2
    depth = arrays[-1].shape[1]
    members = len(copies)
    out = jax.ShapeDtypeStruct((members, rows, 2 * HD), jnp.float32)
    ids = jax.ShapeDtypeStruct((len(pieces), PAD, HD), jnp.bfloat16)
    vmem = pl.BlockSpec(memory_space=pltpu.VMEM)
    rows_of = jax.ShapeDtypeStruct((members * rows, depth), jnp.bfloat16)
    results = [out] * (3 if early else 2) + [ids] + [rows_of] * early
    return pl.pallas_call(
        functools.partial(head_kernel, [c[:2] for c in copies], heads, early),
        in_specs=[pl.BlockSpec(memory_space=pltpu.SMEM)]
        + [pl.BlockSpec(memory_space=pl.ANY)] * (len(arrays) + len(pieces))
        + [vmem] * len(held),
        out_specs=[vmem] * len(results),
        out_shape=results,
        scratch_shapes=[
            pltpu.VMEM((heads, depth, 2 * HD), jnp.bfloat16),
            pltpu.SemaphoreType.DMA((members + 2 * len(pieces),)),
        ],
        compiler_params=pltpu.CompilerParams(vmem_limit_bytes=24 * MIB),
        cost_estimate=pl.CostEstimate(
            flops=0 if early else 4 * members * rows * depth * heads * HD * 100,
            bytes_accessed=0 if early else 2 * depth * (members * rows + heads * 2 * HD),
            transcendentals=0,
        ),
        name="project_early" if early else "project_late",
    )(table, *arrays, *pieces, *held)


def share_kernel(mine_ref, got_ref, own_ref, *out_refs):
    own_ref[...] = mine_ref[0] + got_ref[0]
    for k, out_ref in enumerate(out_refs):
        total = mine_ref[k + 1] + got_ref[k + 1]
        out_ref[:, : 2 * HD] = total.astype(jnp.bfloat16)
        keys = total[:, :HD]
        rest = keys - keys.astype(jnp.bfloat16).astype(jnp.float32)
        out_ref[:, 2 * HD :] = rest.astype(jnp.bfloat16)


def shares(mine, got):
    members, rows, columns = mine.shape
    out = jax.ShapeDtypeStruct((rows, columns + HD), jnp.bfloat16)
    vmem = pl.BlockSpec(memory_space=pltpu.VMEM)
    return pl.pallas_call(
        share_kernel,
        in_specs=[vmem] * 2,
        out_specs=[vmem] * members,
        out_shape=[jax.ShapeDtypeStruct((rows, columns), jnp.float32)] + [out] * (members - 1),
        compiler_params=pltpu.CompilerParams(vmem_limit_bytes=16 * MIB),
        name="shares",
    )(mine, got)


def sum_kernel(place_ref, *refs):
    out_ref = refs[-1]
    for k, group in enumerate((refs[:4], refs[4:8])):
        keys, values = group[0][:, :HD], group[0][:, HD:]
        for ref in group[1:]:
            rest = ref[:, 2 * HD :].astype(jnp.float32)
            keys = keys + (ref[:, :HD].astype(jnp.float32) + rest)
            values = values + ref[:, HD : 2 * HD].astype(jnp.float32)
        first = pl.multiple_of(jnp.bitwise_xor(place_ref[0], k) * 2 * HD, 2 * HD)
        out_ref[:, pl.ds(first, HD)] = keys.astype(jnp.bfloat16)
        out_ref[:, pl.ds(pl.multiple_of(first + HD, HD), HD)] = values.astype(jnp.bfloat16)


def summed(zz, straight, flipped):
    rows = straight[0].shape[0]
    vmem = pl.BlockSpec(memory_space=pltpu.VMEM)
    return pl.pallas_call(
        sum_kernel,
        in_specs=[pl.BlockSpec(memory_space=pltpu.SMEM)] + [vmem] * 8,
        out_specs=vmem,
        out_shape=jax.ShapeDtypeStruct((rows, 4 * HD), jnp.bfloat16),
        compiler_params=pltpu.CompilerParams(vmem_limit_bytes=16 * MIB),
        name="sum",
    )(zz.astype(jnp.int32)[None], *straight, *flipped)


def keyval_by_steps(sizes, hidden, codes, scales, segment_ids):
    rows = hidden.shape[0]
    hi, zz, y = lax.axis_index("hi"), lax.axis_index("zz"), lax.axis_index("y")
    shard = (hi * 2 + zz) * 2 + y
    same = (hi == lax.axis_index("tensor")).astype(jnp.int32)
    arrays, copies, piece = gather_by_steps(sizes, hidden, codes, scales, segment_ids)
    numbers = [c[2] for c in copies] + [y, same]
    table = jnp.stack([jnp.asarray(n, jnp.int32) for n in numbers])
    swap = flat_pairs(sizes, lambda g, s, c: (g, s, 1 - c))
    over_z = flat_pairs(sizes, lambda g, s, c: (g, s ^ 2, c))
    over_x = flat_pairs(sizes, lambda g, s, c: (1 - g, s, c))
    over_both = flat_pairs(sizes, lambda g, s, c: (1 - g, s ^ 2, c))

    def exchanged(mine, other):
        own, to_z, to_x, to_both = shares(mine, lax.ppermute(other, ALL, swap))
        return (
            own,
            lax.ppermute(to_both, ALL, over_both),
            lax.ppermute(to_z, ALL, over_z),
            lax.ppermute(to_x, ALL, over_x),
        )

    order = (2, 3, 6, 7, 0, 1)
    mine, other, own, ids, left = project_heads(
        True, arrays, copies, [piece[d] for d in order], table, rows
    )
    flipped = exchanged(mine, other)
    mine, other, last = project_heads(
        False, arrays, copies, [piece[4], piece[5]], table, rows, (own, left)
    )
    straight = exchanged(mine, other)
    keyval = summed(
        zz,
        (straight[0], flipped[1], flipped[2], straight[3]),
        (flipped[0], straight[1], straight[2], flipped[3]),
    )
    known = jnp.concatenate([ids, last], axis=0)[:, 0]
    place = jnp.asarray([(order + (4, 5)).index(d) for d in range(8)], jnp.int32)
    known = known[place[jnp.bitwise_xor(shard, jnp.arange(8, dtype=jnp.int32))]]
    return keyval, known


def gather_whole(sizes, hidden, codes, scales, segment_ids):
    groups = sizes[0]
    pair = lax.axis_size("zz")
    members = groups * pair
    rows, features = hidden.shape
    depth = features // members
    width = codes.shape[1]
    shards = sizes[1]
    shard = lax.axis_index(SHARD)
    share = pair * depth
    sliced = jnp.moveaxis(hidden.reshape(rows, members, depth), 1, 0)
    got = lax.all_to_all(sliced, BLOCK, 0, 0, tiled=True).reshape(members * rows, depth)
    copies = [(0, m * rows, 0, m) for m in range(members)]

    blocks = share // BLK
    group = lax.axis_index("groups")
    column = lax.dynamic_slice_in_dim(scales, (shard * width) // BLK, 1, 1)
    column = lax.dynamic_slice_in_dim(column, group * blocks, blocks, 0)
    held = lax.dynamic_slice_in_dim(codes, group * share, share, 0)
    weight = (held.astype(jnp.float32).reshape(blocks, BLK, width) * column[:, :, None]).astype(
        jnp.bfloat16
    )
    weight = weight.reshape(pair, depth, width)
    ids = segment_ids.astype(jnp.bfloat16).reshape(rows // width, width)
    ids = jnp.pad(ids, ((0, PAD - rows // width), (0, 0)))
    weight = jnp.concatenate([weight, jnp.broadcast_to(ids, (pair, PAD, width))], axis=1)
    high = lax.axis_size("hi")
    weight = jnp.broadcast_to(weight[None], (high,) + weight.shape)
    weight = weight.reshape(high * pair, depth + PAD, width)
    weight = lax.all_to_all(weight, ("hi", "zz"), 0, 0, tiled=True)
    weight = lax.all_gather(weight, "y", axis=1).reshape(shards, depth + PAD, width)
    known = weight[:, depth : depth + rows // width, :].reshape(shards, rows)
    weight = jnp.moveaxis(weight[:, :depth].reshape(2, shards // 2, depth, width), 1, 2)
    halves = weight.reshape(2, depth, shards * width // 2)
    return [got], copies, [halves[0], halves[1]], jnp.arange(2, dtype=jnp.int32), known


def project_kernel(copies, sources, columns, rows_ref, first_ref, member_ref, shard_ref, core_ref, *refs):
    hidden_refs, refs = refs[:sources], refs[sources:]
    weight_refs, (other_ref, mine_ref, left, halves, sems) = refs[:-5], refs[-5:]
    step = pl.program_id(0)
    rows = mine_ref.shape[1]
    depth = left.shape[1]
    core = core_ref[0]

    @pl.when(step == 0)
    def _():
        started = []
        for k, at in enumerate(copies):
            first = pl.multiple_of(first_ref[k], 128)
            row = pl.multiple_of(rows_ref[k], 16)
            to = pl.multiple_of(member_ref[k] * rows, rows)
            started.append(
                pltpu.make_async_copy(
                    hidden_refs[at].at[pl.ds(row, rows), pl.ds(first, depth)],
                    left.at[pl.ds(to, rows), :],
                    sems.at[k],
                )
            )
        for k, ref in enumerate(weight_refs):
            width = ref.shape[1]
            first = shard_ref[k] * width
            half = jnp.bitwise_xor(core, first // columns)
            at = pl.multiple_of(first % columns, 128)
            started.append(
                pltpu.make_async_copy(
                    ref.at[pl.ds(0, depth), :],
                    halves.at[half, :, pl.ds(at, width)],
                    sems.at[len(copies) + k],
                )
            )
        for copy in started:
            copy.start()
        for copy in started:
            copy.wait()

    size = mine_ref.shape[2]
    per_half = columns // size
    for half, out_ref in ((1, other_ref), (0, mine_ref)):
        for k in range(per_half):

            @pl.when(step == (1 - half) * per_half + k)
            def _():
                total = jnp.dot(
                    left[...],
                    halves[half, :, k * size : (k + 1) * size],
                    preferred_element_type=jnp.float32,
                )
                out_ref[...] = total.reshape(out_ref.shape)


def project(arrays, copies, pieces, shards, core, rows):
    members = len(copies)
    width = pieces[0].shape[1]
    columns = len(pieces) * width // 2
    depth = arrays[-1].shape[1]
    table = [jnp.stack([jnp.asarray(c[i], jnp.int32) for c in copies]) for i in (1, 2, 3)]
    size = 256
    per_half = columns // size
    out = jax.ShapeDtypeStruct((members, rows, columns), jnp.float32)
    return pl.pallas_call(
        functools.partial(project_kernel, [c[0] for c in copies], len(arrays), columns),
        grid_spec=pltpu.PrefetchScalarGridSpec(
            num_scalar_prefetch=5,
            grid=(2 * per_half,),
            in_specs=[pl.BlockSpec(memory_space=pl.ANY)] * (len(arrays) + len(pieces)),
            out_specs=[
                pl.BlockSpec((members, rows, size), lambda i, *_: (0, 0, jnp.minimum(i, per_half - 1))),
                pl.BlockSpec((members, rows, size), lambda i, *_: (0, 0, jnp.maximum(i - per_half, 0))),
            ],
            scratch_shapes=[
                pltpu.VMEM((members * rows, depth), jnp.bfloat16),
                pltpu.VMEM((2, depth, columns), jnp.bfloat16),
                pltpu.SemaphoreType.DMA((len(copies) + len(pieces),)),
            ],
        ),
        out_shape=[out, out],
        compiler_params=pltpu.CompilerParams(vmem_limit_bytes=24 * MIB),
        name="project",
    )(*table, shards, core, *arrays, *pieces)


def split_kernel(mine_ref, got_ref, out_ref):
    total = mine_ref[...] + got_ref[...]
    columns = total.shape[2]
    out_ref[:, :, :columns] = total.astype(jnp.bfloat16)
    for head in range(columns // (2 * HD)):
        keys = total[:, :, 2 * head * HD : (2 * head + 1) * HD]
        rest = keys - keys.astype(jnp.bfloat16).astype(jnp.float32)
        at = columns + head * HD
        out_ref[:, :, at : at + HD] = rest.astype(jnp.bfloat16)


def split(mine, got):
    members, rows, columns = mine.shape
    spec = pl.BlockSpec((1, rows, columns), lambda i: (i, 0, 0))
    wide = columns + columns // 2
    return pl.pallas_call(
        split_kernel,
        grid=(members,),
        in_specs=[spec, spec],
        out_specs=pl.BlockSpec((1, rows, wide), lambda i: (i, 0, 0)),
        out_shape=jax.ShapeDtypeStruct((members, rows, wide), jnp.bfloat16),
        compiler_params=pltpu.CompilerParams(vmem_limit_bytes=24 * MIB),
        name="split",
    )(mine, got)


def attend_kernel(pieces, heads, stack, query_ref, bias_ref, *refs):
    kv_refs, (out_ref, keys, values) = refs[:pieces], refs[pieces:]
    rows = query_ref.shape[0]
    scaling = math.log2(math.e) / math.sqrt(HD)
    for d, ref in enumerate(kv_refs):
        keys[d * rows : (d + 1) * rows, :] = ref[:, :HD]
        values[d * rows : (d + 1) * rows, :] = ref[:, HD:]
    bias = jnp.concatenate([bias_ref[...]] * stack, axis=0)
    for part in range(heads // stack):
        columns = [slice((part * stack + h) * HD, (part * stack + h + 1) * HD) for h in range(stack)]
        query = jnp.concatenate([query_ref[:, c] for c in columns], axis=0)
        scores = lax.dot_general(
            query, keys[...], (((1,), (1,)), ((), ())), preferred_element_type=jnp.float32
        )
        scores = scores + bias
        weights = jnp.exp2((scores - jnp.max(scores, axis=1, keepdims=True)) * scaling)
        totals = jnp.sum(weights, axis=1, keepdims=True)
        result = jnp.dot(
            weights.astype(jnp.bfloat16), values[...], preferred_element_type=jnp.float32
        )
        result = (result / totals).astype(jnp.bfloat16)
        for h, c in enumerate(columns):
            out_ref[:, c] = result[h * rows : (h + 1) * rows]


def attend(queries, bias, pieces):
    rows, width = queries.shape
    window = bias.shape[1]
    group = QPK * HD
    stack = 4 if window <= 1024 else 1
    return pl.pallas_call(
        functools.partial(attend_kernel, len(pieces), QPK, stack),
        grid=(width // group,),
        in_specs=[
            pl.BlockSpec((rows, group), lambda i: (0, i)),
            pl.BlockSpec((rows, window), lambda i: (0, 0)),
        ]
        + [pl.BlockSpec((rows, 2 * HD), lambda i: (0, i))] * len(pieces),
        out_specs=pl.BlockSpec((rows, group), lambda i: (0, i)),
        out_shape=jax.ShapeDtypeStruct((rows, width), jnp.bfloat16),
        scratch_shapes=[pltpu.VMEM((window, HD), jnp.bfloat16)] * 2,
        compiler_params=pltpu.CompilerParams(vmem_limit_bytes=24 * MIB),
        name="attend",
    )(queries, bias, *pieces)


def keyval_whole(sizes, hidden, codes, scales, segment_ids):
    rows = hidden.shape[0]
    core = lax.axis_index("tensor").astype(jnp.int32)
    arrays, copies, pieces, where, known = gather_whole(sizes, hidden, codes, scales, segment_ids)
    other, mine = project(arrays, copies, pieces, where, core[None], rows)
    swap = flat_pairs(sizes, lambda g, s, c: (g, s, 1 - c))
    partial = split(mine, lax.ppermute(other, ALL, swap))
    partial = lax.all_to_all(partial, BLOCK, 0, 0, tiled=True)
    total = jnp.sum(partial.astype(jnp.float32), axis=0)
    columns = mine.shape[2]
    rest = total[:, columns:].reshape(rows, -1, 1, HD)
    rest = jnp.concatenate([rest, jnp.zeros_like(rest)], axis=2).reshape(rows, columns)
    return (total[:, :columns] + rest).astype(jnp.bfloat16), known


def on_device(sizes, hidden, codes, scales, queries, segment_ids):
    groups, shards, cores = sizes
    rows = hidden.shape[0]
    shard = lax.axis_index(SHARD)
    by_steps = groups == 2 and shards == 8 and codes.shape[1] == BLK and rows == BLK
    make = keyval_by_steps if by_steps else keyval_whole
    keyval, known = make(sizes, hidden, codes, scales, segment_ids)

    back = min(shards // 2 + 1, shards - 1)
    from_shard = shard - jnp.arange(back + 1, dtype=jnp.int32)
    seen = known[jnp.maximum(from_shard, 0)].reshape(-1)
    offset = jnp.arange(rows, dtype=jnp.int32)
    keypos = (from_shard[:, None] * rows + offset[None, :]).reshape(-1)
    rowpos = shard * rows + offset
    allowed = (
        (segment_ids.astype(jnp.bfloat16)[:, None] == seen[None, :])
        & (keypos[None, :] <= rowpos[:, None])
        & (keypos[None, :] >= 0)
    )
    bias = jnp.where(allowed, 0.0, -jnp.inf).astype(jnp.float32)

    pieces = [keyval]
    for d in range(1, back + 1):
        up = flat_pairs(sizes, lambda g, s, c: (g, s + d, c) if s + d < shards else None)
        pieces.append(lax.ppermute(keyval, ALL, up))
    return attend(queries, bias, pieces)


def solution(mesh):
    sizes = tuple(mesh.shape[name] for name in ("groups", "shard", "tensor"))
    groups, shards, cores = sizes
    y = math.gcd(shards, 2)
    zz = math.gcd(shards // y, 2)
    fine = Mesh(mesh.devices.reshape(groups, shards // (y * zz), zz, y, cores), ALL)
    tokens = ("groups",) + SHARD
    in_specs = (
        P(tokens, "tensor"),
        P("tensor", SHARD),
        P("tensor", None),
        P(tokens, "tensor"),
        P(tokens),
    )
    return jax.shard_map(
        functools.partial(on_device, sizes),
        mesh=fine,
        in_specs=in_specs,
        out_specs=P(tokens, "tensor"),
        check_vma=False,
    )
```
